512 devices in a mesh: path: 16 (over z, core), trade: 32 (over x, y).
Axes of the slice: x: 4, y: 8, z: 8, core: 2. Of those that a mesh axis runs over, the one named last changes fastest.
Arguments:
- basis: bfloat16 [2, 2048, 64], P(None, 'path'), may hold values from -6 to 6
- fx_rates: float32 [2, 2048, 16], P(None, 'path'), may hold values from 0.5 to 2
- coefficients: bfloat16 [64, 131072], P(None, 'trade'), may hold values from -0.375 to 0.375
- unwind_worth_minimum: float32 [131072], P('trade'), may hold values from -0.3 to 0
- position_offset_group: int32 [131072], P('trade'), may hold values from 0 to 2047
- currency: int32 [131072], P('trade'), may hold values from 0 to 15
Outputs:
- exposure: float32 [2, 2048, 2048], P(None, 'path', 'trade')
- expected_exposure: float32 [2, 2048], P(None, 'trade')
The draws below stay inside these ranges and needn't reach their ends.
All inputs are finite; a program needn't handle non-finite values.
Results may differ from the reference program's by a relative error of at most 0.0006.
Values sent between devices are 32-bit elements; how exact they have to be, the bound alone decides.
No kernel may reach another device: no remote copies, remote signals or barrier semaphores. Data moves between devices by JAX's collectives and lax.ppermute only.
A program may use at most 64 MiB of HBM per device.

```python
import math
import jax
import jax.numpy as jnp
from jax import lax

K = 64
NF = 16
DATES = 2
PATHS = 2048
TRADES = 131072
SETS = 2048
N_TRADE = 32


def place_ends(result, stream_key, least, high):
    index_at = [jax.random.randint(jax.random.fold_in(stream_key, axis), (), 0, length) for axis, length in enumerate(result.shape)]
    widest = result.shape.index(max(result.shape))
    next_to = index_at[:widest] + [(index_at[widest] + 1) % result.shape[widest]] + index_at[widest + 1:]
    return result.at[tuple(index_at)].set(least).at[tuple(next_to)].set(high)


def shard_levels(stream_key, shape, cuts, least, high):
    def one(axis_at, parts):
        steps = jax.random.uniform(jax.random.fold_in(jax.random.fold_in(stream_key, 6), axis_at), (parts,), jnp.float32, least / len(cuts), high / len(cuts))
        return jnp.repeat(jnp.exp(steps), shape[axis_at] // parts).reshape((-1,) + (1,) * (len(shape) - axis_at - 1))

    gain = one(*cuts[0])
    for cut in cuts[1:]:
        gain = gain * one(*cut)
    return gain


def centred(stream_key, shape, scale, bound, pieces=(), held_as=jnp.bfloat16):
    factor_of = shard_levels(stream_key, shape, pieces, -0.22, 0.18) if pieces else 1.0
    array = jax.random.normal(stream_key, shape, jnp.float32) * scale * factor_of
    return jnp.minimum(jnp.maximum(array, -bound), bound).astype(held_as)


def setup_inputs(seed: int = 0) -> dict:
    keys = jax.random.split(jax.random.key(seed), 7)
    return {
        "basis": centred(keys[0], (DATES, PATHS, K), 1.0, 6.0, ((1, 16),)),
        "fx_rates": jnp.clip(jnp.exp(math.log(2.0) - 1.3862944 * jax.random.uniform(keys[1], (DATES, PATHS, NF), jnp.float32) ** shard_levels(keys[1], (DATES, PATHS, NF), ((1, 16),), -0.2, 0.2)), 0.5, 2.0),
        "coefficients": centred(keys[2], (K, TRADES), (4 * K) ** -0.5, 0.375, ((1, 32),)),
        "unwind_worth_minimum": jnp.clip(-0.3 + 0.3 * jax.random.uniform(keys[3], (TRADES,), jnp.float32) ** shard_levels(keys[3], (TRADES,), ((0, 32),), -0.2, 0.2), -0.3, 0.0),
        "position_offset_group": place_ends(jax.random.randint(keys[4], (TRADES,), 0, SETS), jax.random.fold_in(keys[4], 1), 0, SETS - 1).astype(jnp.int32),
        "currency": place_ends(jax.random.randint(keys[5], (TRADES,), 0, NF), jax.random.fold_in(keys[5], 1), 0, NF - 1).astype(jnp.int32),
    }


def reference(basis, fx_rates, coefficients, unwind_worth_minimum, position_offset_group, currency):
    highest = lax.Precision.HIGHEST
    basis_wide = basis.astype(jnp.float32)
    gram = jnp.einsum('dpk,dpl->dkl', basis_wide, basis_wide, precision=highest)
    blocks = N_TRADE
    width = TRADES // blocks
    coef_blocks = coefficients.reshape(K, blocks, width).transpose(1, 0, 2)
    exit_blocks = unwind_worth_minimum.reshape(blocks, width)
    set_blocks = position_offset_group.reshape(blocks, width)
    cur_blocks = currency.reshape(blocks, width)

    def accumulate(total, piece):
        coef, exits, sets_here, currency_present = piece
        fitted_regressor_guess = jnp.einsum('dpk,kt->dpt', basis_wide, coef.astype(jnp.float32), precision=highest)
        cur_table = (currency_present[:, None] == jnp.arange(NF, dtype=jnp.int32)[None, :]).astype(jnp.float32)
        market_rate = jnp.einsum('dpf,tf->dpt', fx_rates, cur_table, precision=highest)
        value = (market_rate * jnp.maximum(fitted_regressor_guess, exits[None, None, :])).astype(jnp.bfloat16)
        value = lax.optimization_barrier(value).astype(jnp.float32)
        weighted = jnp.einsum('dpk,dpt->dkt', basis_wide, value, precision=highest)
        set_table = (sets_here[:, None] == jnp.arange(SETS, dtype=jnp.int32)[None, :]).astype(jnp.float32)
        return (total + jnp.einsum('dkt,ts->dks', weighted, set_table, precision=highest), None)
    moments, unused = lax.scan(accumulate, jnp.zeros((DATES, K, SETS), jnp.float32), (coef_blocks, exit_blocks, set_blocks, cur_blocks))
    solved_coefficient = []
    for date in range(DATES):
        factor = jnp.linalg.cholesky(gram[date])
        solved_coefficient.append(jax.scipy.linalg.cho_solve((factor, True), moments[date]))
    beta = jnp.stack(solved_coefficient)
    smooth = jnp.einsum('dpk,dks->dps', basis_wide, beta, precision=highest)
    exposure = jnp.maximum(smooth, 0.0)
    expected_exposure = jnp.sum(exposure, axis=1) / PATHS
    return (exposure, expected_exposure)
```

```python
import jax
import jax.numpy as jnp
from jax import lax
from jax.experimental import pallas as pl
from jax.experimental.pallas import tpu as pltpu
from jax.sharding import Mesh, PartitionSpec as P

F32 = jnp.float32
BF16 = jnp.bfloat16
HIGHEST = lax.Precision.HIGHEST
DATES = 2
K = 64
NF = 16
SETS = 2048
PATHS = 2048
OWNERS = 32
SET_DEV = SETS // OWNERS
HALF = SET_DEV // 2
LANES = DATES * K
TILE = 1024
VMEM = pl.BlockSpec(memory_space=pltpu.VMEM)
SMEM = pl.BlockSpec(memory_space=pltpu.SMEM)


def split(x):
    high = x.astype(BF16)
    rest = x - high.astype(F32)
    middle = rest.astype(BF16)
    low = (rest - middle.astype(F32)).astype(BF16)
    return high, middle, low


def dot_nt(a, b, precision=None):
    return lax.dot_general(
        a, b, (((1,), (1,)), ((), ())), precision=precision, preferred_element_type=F32
    )


def dot_tn(a, b, precision=None):
    return lax.dot_general(
        a, b, (((0,), (0,)), ((), ())), precision=precision, preferred_element_type=F32
    )


def block_diagonal(a, b):
    return jnp.concatenate(
        [
            jnp.concatenate([a, jnp.zeros((a.shape[0], b.shape[1]), a.dtype)], axis=1),
            jnp.concatenate([jnp.zeros((b.shape[0], a.shape[1]), b.dtype), b], axis=1),
        ],
        axis=0,
    )


def half_moments(half, basis_ref, value_ref, group_ref, out_ref, total_ref):
    rows = OWNERS * HALF
    trades = value_ref.shape[1]
    for i in range(trades // TILE):
        span = pl.ds(i * TILE, TILE)
        group = group_ref[:, span]
        row = jnp.where(
            (group // HALF) % 2 == half, (group // SET_DEV) * HALF + group % HALF, -1
        )
        member = lax.broadcasted_iota(jnp.int32, (rows, TILE), 0) == row
        part = dot_nt(jnp.where(member, 1.0, 0.0).astype(BF16), value_ref[:, span])
        if i == 0:
            total_ref[...] = part
        else:
            total_ref[...] += part
    wide = block_diagonal(basis_ref[0], basis_ref[1])
    step = 256
    for i in range(rows // step):
        span = pl.ds(i * step, step)
        high, middle, low = split(total_ref[span, :])
        moments = (
            jnp.dot(high, wide, preferred_element_type=F32)
            + jnp.dot(middle, wide, preferred_element_type=F32)
            + jnp.dot(low, wide, preferred_element_type=F32)
        )
        out_ref[pl.ds(i * step // HALF, step // HALF)] = moments.reshape(
            step // HALF, HALF, LANES
        )


def send_kernel(
    core_ref, basis_ref, fx_ref, coef_ref, floor_ref, group_ref, currency_ref,
    out_ref, value_ref, total_ref,
):
    paths = basis_ref.shape[1]
    trades = coef_ref.shape[1]
    basis = basis_ref[...].reshape(DATES * paths, K)
    rates = jnp.concatenate(split(fx_ref[...].reshape(DATES * paths, NF)), axis=1)
    for i in range(trades // TILE):
        span = pl.ds(i * TILE, TILE)
        fitted = jnp.dot(basis, coef_ref[:, span], preferred_element_type=F32)
        names = lax.broadcasted_iota(jnp.int32, (3 * NF, TILE), 0) % NF
        chosen = jnp.where(names == currency_ref[:, span], 1.0, 0.0).astype(BF16)
        rate = jnp.dot(rates, chosen, preferred_element_type=F32)
        value_ref[:, span] = (rate * jnp.maximum(fitted, floor_ref[:, span])).astype(BF16)
    half_moments(1 - core_ref[0], basis_ref, value_ref, group_ref, out_ref, total_ref)


def keep_kernel(core_ref, basis_ref, value_ref, group_ref, out_ref, total_ref):
    half_moments(core_ref[0], basis_ref, value_ref, group_ref, out_ref, total_ref)


def inverse_kernel(near_ref, far_ref, out_ref, wide_ref):
    near = near_ref[...].reshape(PATHS // 2, LANES).astype(BF16)
    far = far_ref[...].reshape(PATHS // 2, LANES).astype(BF16)
    wide_ref[: PATHS // 2, :] = near
    wide_ref[PATHS // 2 :, :] = far
    gram = dot_tn(near, near) + dot_tn(far, far)
    row = lax.broadcasted_iota(jnp.int32, (K, K), 0)
    col = lax.broadcasted_iota(jnp.int32, (K, K), 1)
    eye = jnp.where(row == col, 1.0, 0.0).astype(F32)
    blocks = [
        [
            jnp.concatenate(
                [gram[d * K + i : d * K + i + 8, d * K : d * K + K], eye[i : i + 8]], axis=1
            )
            for i in range(0, K, 8)
        ]
        for d in range(DATES)
    ]
    below = lax.broadcasted_iota(jnp.int32, (8, LANES), 0)
    done = [[], []]
    for j in range(K):
        b, r = j // 8, j % 8
        for d in range(DATES):
            work = blocks[d]
            columns = [
                jnp.broadcast_to(work[i][:, j : j + 1], (8, LANES)) for i in range(b, K // 8)
            ]
            pivot = columns[0][r : r + 1, :]
            pivot_row = work[b][r : r + 1, :]
            done[d].append(pivot_row * lax.rsqrt(pivot))
            scaled = pivot_row / pivot
            for i in range(b, K // 8):
                factor = columns[i - b]
                if i == b:
                    factor = jnp.where(below > r, factor, 0.0)
                work[i] = work[i] - factor * scaled
    inverses = []
    for d in range(DATES):
        factor_inverse = jnp.concatenate(done[d], axis=0)[:, K:]
        inverses.append(dot_tn(factor_inverse, factor_inverse, HIGHEST))
    out_ref[...] = block_diagonal(*inverses)


def exposure_kernel(
    parts_ref, inverse_ref, basis_ref, wide_ref, exposure_ref, expected_ref
):
    peers = parts_ref.shape[0]
    halves = []
    for h in range(2):
        total = parts_ref[h]
        for i in range(h + 2, peers, 2):
            total = total + parts_ref[i]
        halves.append(total)
    moments = jnp.concatenate(halves, axis=0)
    beta = jnp.dot(moments, inverse_ref[...], precision=HIGHEST, preferred_element_type=F32)
    lane = lax.broadcasted_iota(jnp.int32, (SET_DEV, LANES), 1)
    rows = jnp.concatenate(
        [jnp.where(lane < K, beta, 0.0), jnp.where(lane < K, 0.0, beta)], axis=0
    )
    high, middle, low = split(rows)

    def smooth(basis):
        return dot_nt(basis, high) + dot_nt(basis, middle) + dot_nt(basis, low)

    mine = jnp.concatenate([basis_ref[0], basis_ref[1]], axis=1)
    exposure = jnp.maximum(smooth(mine), 0.0)
    exposure_ref[0] = exposure[:, :SET_DEV]
    exposure_ref[1] = exposure[:, SET_DEV:]
    total = jnp.zeros((8, LANES), F32)
    step = 512
    for i in range(PATHS // step):
        part = jnp.maximum(smooth(wide_ref[pl.ds(i * step, step), :]), 0.0)
        total = total + jnp.sum(part.reshape(step // 8, 8, LANES), axis=0)
    mean = jnp.sum(total, axis=0, keepdims=True) / PATHS
    expected_ref[0:1, :] = mean[:, :SET_DEV]
    expected_ref[1:2, :] = mean[:, SET_DEV:]


def params(**more):
    return pltpu.CompilerParams(vmem_limit_bytes=40 * 2**20, **more)


def shards(basis, fx_rates, coefficients, unwind_worth_minimum, position_offset_group, currency):
    paths = basis.shape[1]
    trades = coefficients.shape[1]
    core = lax.axis_index("core").reshape(1)
    swap = [(0, 1), (1, 0)]
    floor = unwind_worth_minimum.reshape(1, trades)
    group = position_offset_group.reshape(1, trades)
    names = currency.reshape(1, trades)

    flat = jnp.concatenate([basis[0], basis[1]], axis=1).astype(F32)
    near = lax.all_to_all(
        jnp.broadcast_to(flat[None], (lax.axis_size("z"), paths, LANES)), "z", 0, 0, tiled=True
    )

    moment_shape = jax.ShapeDtypeStruct((OWNERS, HALF, LANES), F32)
    total_scratch = pltpu.VMEM((OWNERS * HALF, DATES * paths), F32)
    send, value = pl.pallas_call(
        send_kernel,
        out_shape=(moment_shape, jax.ShapeDtypeStruct((DATES * paths, trades), BF16)),
        in_specs=[SMEM] + [VMEM] * 6,
        out_specs=(VMEM, VMEM),
        scratch_shapes=[total_scratch],
        compiler_params=params(),
        cost_estimate=pl.CostEstimate(
            flops=2 * 256 * 4096 * 1400, bytes_accessed=4 * 2**20, transcendentals=0
        ),
        name="values_and_sent_half",
    )(core, basis, fx_rates, coefficients, floor, group, names)
    received = lax.ppermute(send, "core", swap)
    kept = pl.pallas_call(
        keep_kernel,
        out_shape=moment_shape,
        in_specs=[SMEM] + [VMEM] * 3,
        out_specs=VMEM,
        scratch_shapes=[total_scratch],
        compiler_params=params(),
        cost_estimate=pl.CostEstimate(
            flops=2 * 256 * 4096 * 1024, bytes_accessed=3 * 2**20, transcendentals=0
        ),
        name="kept_half",
    )(core, basis, value, group)
    owned = lax.all_to_all(kept + received, ("x", "y"), 0, 0, tiled=True)

    far = lax.ppermute(near, "core", swap)
    inverse, wide = pl.pallas_call(
        inverse_kernel,
        out_shape=(
            jax.ShapeDtypeStruct((LANES, LANES), F32),
            jax.ShapeDtypeStruct((PATHS, LANES), BF16),
        ),
        in_specs=[VMEM] * 2,
        out_specs=(VMEM, VMEM),
        compiler_params=params(),
        cost_estimate=pl.CostEstimate(
            flops=2 * 2**31, bytes_accessed=2**21, transcendentals=0
        ),
        name="gram_inverse",
    )(near, far)

    summed = jnp.sum(owned, axis=0)
    peers = lax.axis_size("z") * lax.axis_size("core")
    parts = lax.all_to_all(
        jnp.broadcast_to(summed[None], (peers, HALF, LANES)), ("z", "core"), 0, 0, tiled=True
    )
    return pl.pallas_call(
        exposure_kernel,
        out_shape=(
            jax.ShapeDtypeStruct((DATES, paths, SET_DEV), F32),
            jax.ShapeDtypeStruct((DATES, SET_DEV), F32),
        ),
        in_specs=[VMEM] * 4,
        out_specs=(VMEM, VMEM),
        compiler_params=params(),
        name="exposure",
    )(parts, inverse, basis, wide)


def solution(mesh):
    parts = Mesh(mesh.devices.reshape(8, 2, 4, 8), ("z", "core", "x", "y"))
    path, trade = ("z", "core"), ("x", "y")
    return jax.shard_map(
        shards,
        mesh=parts,
        in_specs=(
            P(None, path, None),
            P(None, path, None),
            P(None, trade),
            P(trade),
            P(trade),
            P(trade),
        ),
        out_specs=(P(None, path, trade), P(None, trade)),
        check_vma=False,
    )
```

```python
import jax
import jax.numpy as jnp
from jax import lax
from jax.experimental import pallas as pl
from jax.experimental.pallas import tpu as pltpu
from jax.sharding import Mesh, PartitionSpec as P

F32 = jnp.float32
BF16 = jnp.bfloat16
HIGHEST = lax.Precision.HIGHEST
DATES = 2
K = 64
NF = 16
SETS = 2048
PATHS = 2048
OWNERS = 32
SET_DEV = SETS // OWNERS
HALF = SET_DEV // 2
LANES = DATES * K
TILE = 1024
VMEM = pl.BlockSpec(memory_space=pltpu.VMEM)
SMEM = pl.BlockSpec(memory_space=pltpu.SMEM)


def split(x):
    high = x.astype(BF16)
    rest = x - high.astype(F32)
    middle = rest.astype(BF16)
    low = (rest - middle.astype(F32)).astype(BF16)
    return high, middle, low


def dot_nt(a, b, precision=None):
    return lax.dot_general(
        a, b, (((1,), (1,)), ((), ())), precision=precision, preferred_element_type=F32
    )


def dot_tn(a, b, precision=None):
    return lax.dot_general(
        a, b, (((0,), (0,)), ((), ())), precision=precision, preferred_element_type=F32
    )


def block_diagonal(a, b):
    return jnp.concatenate(
        [
            jnp.concatenate([a, jnp.zeros((a.shape[0], b.shape[1]), a.dtype)], axis=1),
            jnp.concatenate([jnp.zeros((b.shape[0], a.shape[1]), b.dtype), b], axis=1),
        ],
        axis=0,
    )


def half_moments(half, wide, value_ref, group_ref, out_ref, total_ref):
    rows = OWNERS * HALF
    trades = value_ref.shape[1]
    for i in range(trades // TILE):
        span = pl.ds(i * TILE, TILE)
        group = group_ref[:, span]
        row = jnp.where(
            (group // HALF) % 2 == half, (group // SET_DEV) * HALF + group % HALF, -1
        )
        member = lax.broadcasted_iota(jnp.int32, (rows, TILE), 0) == row
        part = dot_nt(jnp.where(member, 1.0, 0.0).astype(BF16), value_ref[:, span])
        if i == 0:
            total_ref[...] = part
        else:
            total_ref[...] += part
    step = 256
    for i in range(rows // step):
        span = pl.ds(i * step, step)
        high, middle, low = split(total_ref[span, :])
        moments = (
            jnp.dot(high, wide, preferred_element_type=F32)
            + jnp.dot(middle, wide, preferred_element_type=F32)
            + jnp.dot(low, wide, preferred_element_type=F32)
        )
        out_ref[pl.ds(i * step // HALF, step // HALF)] = moments.reshape(
            step // HALF, HALF, LANES
        )


def by_path(basis_ref):
    return [basis_ref[d].astype(F32).T.astype(BF16) for d in range(DATES)]


def send_kernel(
    core_ref, basis_ref, fx_ref, coef_ref, floor_ref, group_ref, currency_ref,
    out_ref, value_ref, total_ref,
):
    trades = coef_ref.shape[1]
    parts = by_path(basis_ref)
    basis = jnp.concatenate(parts, axis=0)
    fx = jnp.concatenate([fx_ref[d].T for d in range(DATES)], axis=0)
    rates = jnp.concatenate(split(fx), axis=1)
    for i in range(trades // TILE):
        span = pl.ds(i * TILE, TILE)
        fitted = jnp.dot(basis, coef_ref[:, span], preferred_element_type=F32)
        names = lax.broadcasted_iota(jnp.int32, (3 * NF, TILE), 0) % NF
        chosen = jnp.where(names == currency_ref[:, span], 1.0, 0.0).astype(BF16)
        rate = jnp.dot(rates, chosen, preferred_element_type=F32)
        value_ref[:, span] = (rate * jnp.maximum(fitted, floor_ref[:, span])).astype(BF16)
    wide = block_diagonal(*parts)
    half_moments(1 - core_ref[0], wide, value_ref, group_ref, out_ref, total_ref)


def keep_kernel(core_ref, basis_ref, value_ref, group_ref, out_ref, total_ref):
    wide = block_diagonal(*by_path(basis_ref))
    half_moments(core_ref[0], wide, value_ref, group_ref, out_ref, total_ref)


def eliminate(blocks):
    row = lax.broadcasted_iota(jnp.int32, (8, LANES), 0)
    done = []
    for b in range(K // 8):
        height = K // 8 - b
        columns = [
            [
                jnp.broadcast_to(blocks[i][:, b * 8 + c : b * 8 + c + 1], (8, LANES))
                for i in range(b, K // 8)
            ]
            for c in range(8)
        ]
        rows = [blocks[b][c : c + 1, :] for c in range(8)]
        for c in range(8):
            pivot = columns[c][0][c : c + 1, :]
            inverse = 1.0 / pivot
            done.append(rows[c] * lax.rsqrt(pivot))
            scaled = rows[c] * inverse
            for e in range(c + 1, 8):
                entry = columns[c][0][e : e + 1, :]
                rows[e] = rows[e] - entry * scaled
                ratio = entry * inverse
                for i in range(height):
                    columns[e][i] = columns[e][i] - columns[c][i] * ratio
            for i in range(1, height):
                blocks[b + i] = blocks[b + i] - columns[c][i] * scaled
    return jnp.concatenate(done, axis=0)


def inverse_kernel(near_ref, far_ref, out_ref, wide_ref):
    groups = near_ref.shape[0]
    paths = near_ref.shape[2]
    gram = jnp.zeros((LANES, LANES), F32)
    for i, ref in enumerate((near_ref, far_ref)):
        for z in range(groups):
            at = (i * groups + z) * paths
            wide_ref[:, at : at + paths] = ref[z].astype(BF16)
    every = wide_ref[...]
    gram = dot_nt(every, every)
    row = lax.broadcasted_iota(jnp.int32, (K, K), 0)
    col = lax.broadcasted_iota(jnp.int32, (K, K), 1)
    eye = jnp.where(row == col, 1.0, 0.0).astype(F32)
    inverses = []
    for d in range(DATES):
        blocks = [
            jnp.concatenate(
                [gram[d * K + i : d * K + i + 8, d * K : d * K + K], eye[i : i + 8]], axis=1
            )
            for i in range(0, K, 8)
        ]
        factor_inverse = eliminate(blocks)[:, K:]
        inverses.append(dot_tn(factor_inverse, factor_inverse, HIGHEST))
    out_ref[...] = block_diagonal(*inverses)


def exposure_kernel(
    parts_ref, inverse_ref, basis_ref, wide_ref, exposure_ref, expected_ref
):
    peers = parts_ref.shape[0]
    halves = []
    for h in range(2):
        total = parts_ref[h]
        for i in range(h + 2, peers, 2):
            total = total + parts_ref[i]
        halves.append(total)
    moments = jnp.concatenate(halves, axis=0)
    beta = jnp.dot(moments, inverse_ref[...], precision=HIGHEST, preferred_element_type=F32)
    lane = lax.broadcasted_iota(jnp.int32, (SET_DEV, LANES), 1)
    rows = jnp.concatenate(
        [jnp.where(lane < K, beta, 0.0), jnp.where(lane < K, 0.0, beta)], axis=0
    )
    stacked = jnp.concatenate(split(rows), axis=0)

    def exposed(basis):
        smooth = jnp.dot(stacked, basis, preferred_element_type=F32)
        return jnp.maximum(
            smooth[:LANES] + smooth[LANES : 2 * LANES] + smooth[2 * LANES :], 0.0
        )

    paths = basis_ref.shape[2]
    exposure = exposed(basis_ref[...].reshape(LANES, paths))
    exposure_ref[...] = exposure.reshape(DATES, SET_DEV, paths)
    total = jnp.zeros((LANES, 128), F32)
    step = 512
    for i in range(PATHS // step):
        part = exposed(wide_ref[:, i * step : (i + 1) * step])
        for j in range(step // 128):
            total = total + part[:, j * 128 : (j + 1) * 128]
    mean = jnp.sum(total.T, axis=0, keepdims=True) / PATHS
    expected_ref[0:1, :] = mean[:, :SET_DEV]
    expected_ref[1:2, :] = mean[:, SET_DEV:]


def params(**more):
    return pltpu.CompilerParams(vmem_limit_bytes=40 * 2**20, **more)


def shards(basis, fx_rates, coefficients, unwind_worth_minimum, position_offset_group, currency):
    paths = basis.shape[1]
    trades = coefficients.shape[1]
    core = lax.axis_index("core").reshape(1)
    swap = [(0, 1), (1, 0)]
    floor = unwind_worth_minimum.reshape(1, trades)
    group = position_offset_group.reshape(1, trades)
    names = currency.reshape(1, trades)
    basis = jnp.swapaxes(basis, 1, 2)
    fx_rates = jnp.swapaxes(fx_rates, 1, 2)
    flat = basis.reshape(LANES, paths).astype(F32)

    moment_shape = jax.ShapeDtypeStruct((OWNERS, HALF, LANES), F32)
    total_scratch = pltpu.VMEM((OWNERS * HALF, DATES * paths), F32)
    send, value = pl.pallas_call(
        send_kernel,
        out_shape=(moment_shape, jax.ShapeDtypeStruct((DATES * paths, trades), BF16)),
        in_specs=[SMEM] + [VMEM] * 6,
        out_specs=(VMEM, VMEM),
        scratch_shapes=[total_scratch],
        compiler_params=params(),
        cost_estimate=pl.CostEstimate(
            flops=2 * 256 * 4096 * 1400, bytes_accessed=4 * 2**20, transcendentals=0
        ),
        name="values_and_sent_half",
    )(core, basis, fx_rates, coefficients, floor, group, names)
    received = lax.ppermute(send, "core", swap)
    kept = pl.pallas_call(
        keep_kernel,
        out_shape=moment_shape,
        in_specs=[SMEM] + [VMEM] * 3,
        out_specs=VMEM,
        scratch_shapes=[total_scratch],
        compiler_params=params(),
        cost_estimate=pl.CostEstimate(
            flops=2 * 256 * 4096 * 1024, bytes_accessed=3 * 2**20, transcendentals=0
        ),
        name="kept_half",
    )(core, basis, value, group)
    pair = kept + received

    flat, pair = lax.optimization_barrier((flat, pair))
    owned = lax.all_to_all(pair, ("x", "y"), 0, 0, tiled=True)
    near = lax.all_to_all(
        jnp.broadcast_to(flat[None], (lax.axis_size("z"), LANES, paths)), "z", 0, 0, tiled=True
    )

    far = lax.ppermute(near, "core", swap)
    inverse, wide = pl.pallas_call(
        inverse_kernel,
        out_shape=(
            jax.ShapeDtypeStruct((LANES, LANES), F32),
            jax.ShapeDtypeStruct((LANES, PATHS), BF16),
        ),
        in_specs=[VMEM] * 2,
        out_specs=(VMEM, VMEM),
        compiler_params=params(),
        cost_estimate=pl.CostEstimate(
            flops=2 * 2**31, bytes_accessed=2**21, transcendentals=0
        ),
        name="gram_inverse",
    )(near, far)

    summed = jnp.sum(owned, axis=0)
    peers = lax.axis_size("z") * lax.axis_size("core")
    parts = lax.all_to_all(
        jnp.broadcast_to(summed[None], (peers, HALF, LANES)), ("z", "core"), 0, 0, tiled=True
    )
    exposure, expected = pl.pallas_call(
        exposure_kernel,
        out_shape=(
            jax.ShapeDtypeStruct((DATES, SET_DEV, paths), F32),
            jax.ShapeDtypeStruct((DATES, SET_DEV), F32),
        ),
        in_specs=[VMEM] * 4,
        out_specs=(VMEM, VMEM),
        compiler_params=params(),
        name="exposure",
    )(parts, inverse, basis, wide)
    return jnp.swapaxes(exposure, 1, 2), expected


def solution(mesh):
    parts = Mesh(mesh.devices.reshape(8, 2, 4, 8), ("z", "core", "x", "y"))
    path, trade = ("z", "core"), ("x", "y")
    return jax.shard_map(
        shards,
        mesh=parts,
        in_specs=(
            P(None, path, None),
            P(None, path, None),
            P(None, trade),
            P(trade),
            P(trade),
            P(trade),
        ),
        out_specs=(P(None, path, trade), P(None, trade)),
        check_vma=False,
    )
```

```python
import jax
import jax.numpy as jnp
from jax import lax
from jax.experimental import pallas as pl
from jax.experimental.pallas import tpu as pltpu
from jax.sharding import Mesh, PartitionSpec as P

F32 = jnp.float32
BF16 = jnp.bfloat16
HIGHEST = lax.Precision.HIGHEST
DATES = 2
K = 64
NF = 16
SETS = 2048
PATHS = 2048
OWNERS = 32
SET_DEV = SETS // OWNERS
HALF = SET_DEV // 2
LANES = DATES * K
TILE = 1024
VMEM = pl.BlockSpec(memory_space=pltpu.VMEM)
SMEM = pl.BlockSpec(memory_space=pltpu.SMEM)


def split(x):
    high = x.astype(BF16)
    rest = x - high.astype(F32)
    middle = rest.astype(BF16)
    low = (rest - middle.astype(F32)).astype(BF16)
    return high, middle, low


def dot_nt(a, b, precision=None):
    return lax.dot_general(
        a, b, (((1,), (1,)), ((), ())), precision=precision, preferred_element_type=F32
    )


def dot_tn(a, b, precision=None):
    return lax.dot_general(
        a, b, (((0,), (0,)), ((), ())), precision=precision, preferred_element_type=F32
    )


def block_diagonal(a, b):
    return jnp.concatenate(
        [
            jnp.concatenate([a, jnp.zeros((a.shape[0], b.shape[1]), a.dtype)], axis=1),
            jnp.concatenate([jnp.zeros((b.shape[0], a.shape[1]), b.dtype), b], axis=1),
        ],
        axis=0,
    )


def half_moments(half, wide, value_ref, group_ref, out_ref, total_ref):
    rows = OWNERS * HALF
    trades = value_ref.shape[1]
    for i in range(trades // TILE):
        span = pl.ds(i * TILE, TILE)
        group = group_ref[:, span]
        row = jnp.where(
            (group // HALF) % 2 == half, (group // SET_DEV) * HALF + group % HALF, -1
        )
        member = lax.broadcasted_iota(jnp.int32, (rows, TILE), 0) == row
        part = dot_nt(jnp.where(member, 1.0, 0.0).astype(BF16), value_ref[:, span])
        if i == 0:
            total_ref[...] = part
        else:
            total_ref[...] += part
    step = 256
    for i in range(rows // step):
        span = pl.ds(i * step, step)
        high, middle, low = split(total_ref[span, :])
        moments = (
            jnp.dot(high, wide, preferred_element_type=F32)
            + jnp.dot(middle, wide, preferred_element_type=F32)
            + jnp.dot(low, wide, preferred_element_type=F32)
        )
        out_ref[pl.ds(i * step // HALF, step // HALF)] = moments.reshape(
            step // HALF, HALF, LANES
        )


def by_path(basis_ref):
    return [basis_ref[d].astype(F32).T.astype(BF16) for d in range(DATES)]


def send_kernel(
    core_ref, basis_ref, fx_ref, coef_ref, floor_ref, group_ref, currency_ref,
    out_ref, value_ref, total_ref,
):
    trades = coef_ref.shape[1]
    parts = by_path(basis_ref)
    basis = jnp.concatenate(parts, axis=0)
    fx = jnp.concatenate([fx_ref[d].T for d in range(DATES)], axis=0)
    rates = jnp.concatenate(split(fx), axis=1)
    for i in range(trades // TILE):
        span = pl.ds(i * TILE, TILE)
        fitted = jnp.dot(basis, coef_ref[:, span], preferred_element_type=F32)
        names = lax.broadcasted_iota(jnp.int32, (3 * NF, TILE), 0) % NF
        chosen = jnp.where(names == currency_ref[:, span], 1.0, 0.0).astype(BF16)
        rate = jnp.dot(rates, chosen, preferred_element_type=F32)
        value_ref[:, span] = (rate * jnp.maximum(fitted, floor_ref[:, span])).astype(BF16)
    wide = block_diagonal(*parts)
    half_moments(1 - core_ref[0], wide, value_ref, group_ref, out_ref, total_ref)


def keep_kernel(core_ref, basis_ref, value_ref, group_ref, out_ref, total_ref):
    wide = block_diagonal(*by_path(basis_ref))
    half_moments(core_ref[0], wide, value_ref, group_ref, out_ref, total_ref)


def eliminate(blocks):
    row = lax.broadcasted_iota(jnp.int32, (8, LANES), 0)
    done = []
    for b in range(K // 8):
        height = K // 8 - b
        columns = [
            [
                jnp.broadcast_to(blocks[i][:, b * 8 + c : b * 8 + c + 1], (8, LANES))
                for i in range(b, K // 8)
            ]
            for c in range(8)
        ]
        rows = [blocks[b][c : c + 1, :] for c in range(8)]
        for c in range(8):
            pivot = columns[c][0][c : c + 1, :]
            inverse = 1.0 / pivot
            done.append(rows[c] * lax.rsqrt(pivot))
            scaled = rows[c] * inverse
            for e in range(c + 1, 8):
                entry = columns[c][0][e : e + 1, :]
                rows[e] = rows[e] - entry * scaled
                ratio = entry * inverse
                for i in range(height):
                    columns[e][i] = columns[e][i] - columns[c][i] * ratio
            for i in range(1, height):
                blocks[b + i] = blocks[b + i] - columns[c][i] * scaled
    return jnp.concatenate(done, axis=0)


def inverse_kernel(near_ref, far_ref, out_ref, wide_ref):
    groups = near_ref.shape[0]
    paths = near_ref.shape[2]
    gram = jnp.zeros((LANES, LANES), F32)
    for i, ref in enumerate((near_ref, far_ref)):
        for z in range(groups):
            at = (i * groups + z) * paths
            wide_ref[:, at : at + paths] = ref[z].astype(BF16)
    every = wide_ref[...]
    gram = dot_nt(every, every)
    row = lax.broadcasted_iota(jnp.int32, (K, K), 0)
    col = lax.broadcasted_iota(jnp.int32, (K, K), 1)
    eye = jnp.where(row == col, 1.0, 0.0).astype(F32)
    inverses = []
    for d in range(DATES):
        blocks = [
            jnp.concatenate(
                [gram[d * K + i : d * K + i + 8, d * K : d * K + K], eye[i : i + 8]], axis=1
            )
            for i in range(0, K, 8)
        ]
        factor_inverse = eliminate(blocks)[:, K:]
        inverses.append(dot_tn(factor_inverse, factor_inverse, HIGHEST))
    out_ref[...] = block_diagonal(*inverses)


def exposure_kernel(
    parts_ref, inverse_ref, basis_ref, wide_ref, exposure_ref, expected_ref
):
    peers = parts_ref.shape[0]
    halves = []
    for h in range(2):
        total = parts_ref[h]
        for i in range(h + 2, peers, 2):
            total = total + parts_ref[i]
        halves.append(total)
    moments = jnp.concatenate(halves, axis=0)
    beta = jnp.dot(moments, inverse_ref[...], precision=HIGHEST, preferred_element_type=F32)
    lane = lax.broadcasted_iota(jnp.int32, (SET_DEV, LANES), 1)
    rows = jnp.concatenate(
        [jnp.where(lane < K, beta, 0.0), jnp.where(lane < K, 0.0, beta)], axis=0
    )
    stacked = jnp.concatenate(split(rows), axis=0)

    def exposed(basis):
        smooth = jnp.dot(stacked, basis, preferred_element_type=F32)
        return jnp.maximum(
            smooth[:LANES] + smooth[LANES : 2 * LANES] + smooth[2 * LANES :], 0.0
        )

    paths = basis_ref.shape[2]
    exposure = exposed(basis_ref[...].reshape(LANES, paths))
    exposure_ref[...] = exposure.reshape(DATES, SET_DEV, paths)
    total = jnp.zeros((LANES, 128), F32)
    step = 512
    for i in range(PATHS // step):
        part = exposed(wide_ref[:, i * step : (i + 1) * step])
        for j in range(step // 128):
            total = total + part[:, j * 128 : (j + 1) * 128]
    mean = jnp.sum(total.T, axis=0, keepdims=True) / PATHS
    expected_ref[0:1, :] = mean[:, :SET_DEV]
    expected_ref[1:2, :] = mean[:, SET_DEV:]


def params(**more):
    return pltpu.CompilerParams(vmem_limit_bytes=40 * 2**20, **more)


def shards(basis, fx_rates, coefficients, unwind_worth_minimum, position_offset_group, currency):
    paths = basis.shape[1]
    trades = coefficients.shape[1]
    core = lax.axis_index("core").reshape(1)
    swap = [(0, 1), (1, 0)]
    floor = unwind_worth_minimum.reshape(1, trades)
    group = position_offset_group.reshape(1, trades)
    names = currency.reshape(1, trades)
    basis = jnp.swapaxes(basis, 1, 2)
    fx_rates = jnp.swapaxes(fx_rates, 1, 2)
    flat = basis.reshape(LANES, paths).astype(F32)

    near = lax.all_to_all(
        jnp.broadcast_to(flat[None], (lax.axis_size("z"), LANES, paths)), "z", 0, 0, tiled=True
    )

    moment_shape = jax.ShapeDtypeStruct((OWNERS, HALF, LANES), F32)
    total_scratch = pltpu.VMEM((OWNERS * HALF, DATES * paths), F32)
    send, value = pl.pallas_call(
        send_kernel,
        out_shape=(moment_shape, jax.ShapeDtypeStruct((DATES * paths, trades), BF16)),
        in_specs=[SMEM] + [VMEM] * 6,
        out_specs=(VMEM, VMEM),
        scratch_shapes=[total_scratch],
        compiler_params=params(),
        cost_estimate=pl.CostEstimate(
            flops=2 * 256 * 4096 * 1400, bytes_accessed=4 * 2**20, transcendentals=0
        ),
        name="values_and_sent_half",
    )(core, basis, fx_rates, coefficients, floor, group, names)
    received = lax.ppermute(send, "core", swap)
    kept = pl.pallas_call(
        keep_kernel,
        out_shape=moment_shape,
        in_specs=[SMEM] + [VMEM] * 3,
        out_specs=VMEM,
        scratch_shapes=[total_scratch],
        compiler_params=params(),
        cost_estimate=pl.CostEstimate(
            flops=2 * 256 * 4096 * 1024, bytes_accessed=3 * 2**20, transcendentals=0
        ),
        name="kept_half",
    )(core, basis, value, group)
    pair = kept + received
    owned = lax.all_to_all(pair, ("x", "y"), 0, 0, tiled=True)

    far = lax.ppermute(near, "core", swap)
    inverse, wide = pl.pallas_call(
        inverse_kernel,
        out_shape=(
            jax.ShapeDtypeStruct((LANES, LANES), F32),
            jax.ShapeDtypeStruct((LANES, PATHS), BF16),
        ),
        in_specs=[VMEM] * 2,
        out_specs=(VMEM, VMEM),
        compiler_params=params(),
        cost_estimate=pl.CostEstimate(
            flops=2 * 2**31, bytes_accessed=2**21, transcendentals=0
        ),
        name="gram_inverse",
    )(near, far)

    summed = jnp.sum(owned, axis=0)
    inverse, summed = lax.optimization_barrier((inverse, summed))
    peers = lax.axis_size("z") * lax.axis_size("core")
    parts = lax.all_to_all(
        jnp.broadcast_to(summed[None], (peers, HALF, LANES)), ("z", "core"), 0, 0, tiled=True
    )
    exposure, expected = pl.pallas_call(
        exposure_kernel,
        out_shape=(
            jax.ShapeDtypeStruct((DATES, SET_DEV, paths), F32),
            jax.ShapeDtypeStruct((DATES, SET_DEV), F32),
        ),
        in_specs=[VMEM] * 4,
        out_specs=(VMEM, VMEM),
        compiler_params=params(),
        name="exposure",
    )(parts, inverse, basis, wide)
    return jnp.swapaxes(exposure, 1, 2), expected


def solution(mesh):
    parts = Mesh(mesh.devices.reshape(8, 2, 4, 8), ("z", "core", "x", "y"))
    path, trade = ("z", "core"), ("x", "y")
    return jax.shard_map(
        shards,
        mesh=parts,
        in_specs=(
            P(None, path, None),
            P(None, path, None),
            P(None, trade),
            P(trade),
            P(trade),
            P(trade),
        ),
        out_specs=(P(None, path, trade), P(None, trade)),
        check_vma=False,
    )
```

```python
import jax
import jax.numpy as jnp
from jax import lax
from jax.experimental import pallas as pl
from jax.experimental.pallas import tpu as pltpu
from jax.sharding import Mesh, PartitionSpec as P

F32 = jnp.float32
BF16 = jnp.bfloat16
HIGHEST = lax.Precision.HIGHEST
DATES = 2
K = 64
NF = 16
SETS = 2048
PATHS = 2048
OWNERS = 32
SET_DEV = SETS // OWNERS
HALF = SET_DEV // 2
LANES = DATES * K
TILE = 1024
VMEM = pl.BlockSpec(memory_space=pltpu.VMEM)
ANY = pl.BlockSpec(memory_space=pl.ANY)
SMEM = pl.BlockSpec(memory_space=pltpu.SMEM)


def split(x):
    high = x.astype(BF16)
    rest = x - high.astype(F32)
    middle = rest.astype(BF16)
    low = (rest - middle.astype(F32)).astype(BF16)
    return high, middle, low


def dot_nt(a, b, precision=None):
    return lax.dot_general(
        a, b, (((1,), (1,)), ((), ())), precision=precision, preferred_element_type=F32
    )


def dot_tn(a, b, precision=None):
    return lax.dot_general(
        a, b, (((0,), (0,)), ((), ())), precision=precision, preferred_element_type=F32
    )


def block_diagonal(a, b):
    return jnp.concatenate(
        [
            jnp.concatenate([a, jnp.zeros((a.shape[0], b.shape[1]), a.dtype)], axis=1),
            jnp.concatenate([jnp.zeros((b.shape[0], a.shape[1]), b.dtype), b], axis=1),
        ],
        axis=0,
    )


def net_half(half, value_ref, group_ref, total_ref):
    rows = OWNERS * HALF
    trades = value_ref.shape[1]
    for i in range(trades // TILE):
        span = pl.ds(i * TILE, TILE)
        group = group_ref[:, span]
        row = jnp.where(
            (group // HALF) % 2 == half, (group // SET_DEV) * HALF + group % HALF, -1
        )
        member = lax.broadcasted_iota(jnp.int32, (rows, TILE), 0) == row
        part = dot_nt(jnp.where(member, 1.0, 0.0).astype(BF16), value_ref[:, span])
        if i == 0:
            total_ref[...] = part
        else:
            total_ref[...] += part


def half_moments(wide, total_ref, store):
    step = 256
    for i in range(OWNERS * HALF // step):
        span = pl.ds(i * step, step)
        high, middle, low = split(total_ref[span, :])
        moments = (
            jnp.dot(high, wide, preferred_element_type=F32)
            + jnp.dot(middle, wide, preferred_element_type=F32)
            + jnp.dot(low, wide, preferred_element_type=F32)
        )
        store(i * step // HALF, moments.reshape(step // HALF, HALF, LANES))


def payload_kernel(basis_ref, out_ref, narrow_ref, wide_ref, in_sem, out_sems):
    load = pltpu.make_async_copy(basis_ref, narrow_ref, in_sem)
    load.start()
    load.wait()
    wide_ref[...] = narrow_ref[...].reshape(wide_ref.shape).astype(F32)
    copies = [
        pltpu.make_async_copy(wide_ref, out_ref.at[i], out_sems.at[i])
        for i in range(out_ref.shape[0])
    ]
    for copy in copies:
        copy.start()
    for copy in copies:
        copy.wait()


def by_path(basis_ref):
    return [basis_ref[d].astype(F32).T.astype(BF16) for d in range(DATES)]


def send_kernel(
    core_ref, basis_hbm, fx_hbm, coef_hbm, floor_hbm, group_hbm, currency_hbm,
    out_ref, value_ref,
    basis_ref, fx_ref, coef_ref, floor_ref, group_ref, currency_ref, total_ref, sems,
):
    trades = coef_ref.shape[1]
    spans = [pl.ds(i * TILE, TILE) for i in range(trades // TILE)]
    pairs = [
        (basis_hbm, basis_ref), (fx_hbm, fx_ref), (currency_hbm, currency_ref),
        (floor_hbm, floor_ref), (group_hbm, group_ref),
    ]
    pairs[1:1] = [(coef_hbm.at[:, span], coef_ref.at[:, span]) for span in spans]
    copies = [
        pltpu.make_async_copy(source, target, sems.at[i])
        for i, (source, target) in enumerate(pairs)
    ]
    for copy in copies:
        copy.start()
    tiles = len(spans)
    copies[0].wait()
    parts = by_path(basis_ref)
    basis = jnp.concatenate(parts, axis=0)
    for copy in copies[tiles + 1 : tiles + 4]:
        copy.wait()
    fx = jnp.concatenate([fx_ref[d].T for d in range(DATES)], axis=0)
    rates = jnp.concatenate(split(fx), axis=1)
    for i, span in enumerate(spans):
        copies[1 + i].wait()
        fitted = jnp.dot(basis, coef_ref[:, span], preferred_element_type=F32)
        names = lax.broadcasted_iota(jnp.int32, (3 * NF, TILE), 0) % NF
        chosen = jnp.where(names == currency_ref[:, span], 1.0, 0.0).astype(BF16)
        rate = jnp.dot(rates, chosen, preferred_element_type=F32)
        value_ref[:, span] = (rate * jnp.maximum(fitted, floor_ref[:, span])).astype(BF16)
    copies[tiles + 4].wait()

    def store(at, moments):
        out_ref[pl.ds(at, moments.shape[0])] = moments

    wide = block_diagonal(*parts)
    net_half(1 - core_ref[0], value_ref, group_ref, total_ref)
    half_moments(wide, total_ref, store)


def keep_kernel(core_ref, value_ref, group_hbm, total_ref, group_ref, sem):
    load = pltpu.make_async_copy(group_hbm, group_ref, sem)
    load.start()
    load.wait()
    net_half(core_ref[0], value_ref, group_ref, total_ref)


def pair_kernel(
    basis_hbm, total_ref, received_ref, out_hbm, basis_ref, sum_ref, in_sem, out_sems
):
    load = pltpu.make_async_copy(basis_hbm, basis_ref, in_sem)
    load.start()
    load.wait()
    copies = []

    def store(at, moments):
        span = pl.ds(at, moments.shape[0])
        sum_ref[span] = moments + received_ref[span]
        copies.append(
            pltpu.make_async_copy(sum_ref.at[span], out_hbm.at[span], out_sems.at[len(copies)])
        )
        copies[-1].start()

    half_moments(block_diagonal(*by_path(basis_ref)), total_ref, store)
    for copy in copies:
        copy.wait()


def eliminate(blocks):
    row = lax.broadcasted_iota(jnp.int32, (8, LANES), 0)
    done = []
    for b in range(K // 8):
        height = K // 8 - b
        columns = [
            [
                jnp.broadcast_to(blocks[i][:, b * 8 + c : b * 8 + c + 1], (8, LANES))
                for i in range(b, K // 8)
            ]
            for c in range(8)
        ]
        rows = [blocks[b][c : c + 1, :] for c in range(8)]
        for c in range(8):
            pivot = columns[c][0][c : c + 1, :]
            inverse = 1.0 / pivot
            done.append(rows[c] * lax.rsqrt(pivot))
            scaled = rows[c] * inverse
            for e in range(c + 1, 8):
                entry = columns[c][0][e : e + 1, :]
                rows[e] = rows[e] - entry * scaled
                ratio = entry * inverse
                for i in range(height):
                    columns[e][i] = columns[e][i] - columns[c][i] * ratio
            for i in range(1, height):
                blocks[b + i] = blocks[b + i] - columns[c][i] * scaled
    return jnp.concatenate(done, axis=0)


def inverse_kernel(near_ref, far_ref, out_ref, wide_ref):
    groups = near_ref.shape[0]
    paths = near_ref.shape[2]
    gram = jnp.zeros((LANES, LANES), F32)
    for i, ref in enumerate((near_ref, far_ref)):
        for z in range(groups):
            at = (i * groups + z) * paths
            wide_ref[:, at : at + paths] = ref[z].astype(BF16)
    every = wide_ref[...]
    gram = dot_nt(every, every)
    row = lax.broadcasted_iota(jnp.int32, (K, K), 0)
    col = lax.broadcasted_iota(jnp.int32, (K, K), 1)
    eye = jnp.where(row == col, 1.0, 0.0).astype(F32)
    inverses = []
    for d in range(DATES):
        blocks = [
            jnp.concatenate(
                [gram[d * K + i : d * K + i + 8, d * K : d * K + K], eye[i : i + 8]], axis=1
            )
            for i in range(0, K, 8)
        ]
        factor_inverse = eliminate(blocks)[:, K:]
        inverses.append(dot_tn(factor_inverse, factor_inverse, HIGHEST))
    out_ref[...] = block_diagonal(*inverses)


def exposure_kernel(
    parts_ref, inverse_ref, basis_ref, wide_ref, exposure_ref, expected_ref
):
    peers = parts_ref.shape[0]
    halves = []
    for h in range(2):
        total = parts_ref[h]
        for i in range(h + 2, peers, 2):
            total = total + parts_ref[i]
        halves.append(total)
    moments = jnp.concatenate(halves, axis=0)
    beta = jnp.dot(moments, inverse_ref[...], precision=HIGHEST, preferred_element_type=F32)
    lane = lax.broadcasted_iota(jnp.int32, (SET_DEV, LANES), 1)
    rows = jnp.concatenate(
        [jnp.where(lane < K, beta, 0.0), jnp.where(lane < K, 0.0, beta)], axis=0
    )
    stacked = jnp.concatenate(split(rows), axis=0)

    def exposed(basis):
        smooth = jnp.dot(stacked, basis, preferred_element_type=F32)
        return jnp.maximum(
            smooth[:LANES] + smooth[LANES : 2 * LANES] + smooth[2 * LANES :], 0.0
        )

    paths = basis_ref.shape[2]
    exposure = exposed(basis_ref[...].reshape(LANES, paths))
    exposure_ref[...] = exposure.reshape(DATES, SET_DEV, paths)
    total = jnp.zeros((LANES, 128), F32)
    step = 512
    for i in range(PATHS // step):
        part = exposed(wide_ref[:, i * step : (i + 1) * step])
        for j in range(step // 128):
            total = total + part[:, j * 128 : (j + 1) * 128]
    mean = jnp.sum(total.T, axis=0, keepdims=True) / PATHS
    expected_ref[0:1, :] = mean[:, :SET_DEV]
    expected_ref[1:2, :] = mean[:, SET_DEV:]


def params(**more):
    return pltpu.CompilerParams(vmem_limit_bytes=40 * 2**20, **more)


def shards(basis, fx_rates, coefficients, unwind_worth_minimum, position_offset_group, currency):
    paths = basis.shape[1]
    trades = coefficients.shape[1]
    core = lax.axis_index("core").reshape(1)
    swap = [(0, 1), (1, 0)]
    floor = unwind_worth_minimum.reshape(1, trades)
    group = position_offset_group.reshape(1, trades)
    names = currency.reshape(1, trades)
    basis = jnp.swapaxes(basis, 1, 2)
    fx_rates = jnp.swapaxes(fx_rates, 1, 2)
    payload = pl.pallas_call(
        payload_kernel,
        out_shape=jax.ShapeDtypeStruct((lax.axis_size("z"), LANES, paths), F32),
        in_specs=[ANY],
        out_specs=ANY,
        scratch_shapes=[
            pltpu.VMEM((DATES, K, paths), BF16),
            pltpu.VMEM((LANES, paths), F32),
            pltpu.SemaphoreType.DMA(()),
            pltpu.SemaphoreType.DMA((lax.axis_size("z"),)),
        ],
        compiler_params=params(),
        name="basis_payload",
    )(basis)
    near = lax.all_to_all(payload, "z", 0, 0, tiled=True)

    moment_shape = jax.ShapeDtypeStruct((OWNERS, HALF, LANES), F32)
    basis_scratch = pltpu.VMEM((DATES, K, paths), BF16)
    row_scratch = pltpu.VMEM((1, trades), F32)
    index_scratch = pltpu.VMEM((1, trades), jnp.int32)
    total_scratch = pltpu.VMEM((OWNERS * HALF, DATES * paths), F32)
    send, value = pl.pallas_call(
        send_kernel,
        out_shape=(moment_shape, jax.ShapeDtypeStruct((DATES * paths, trades), BF16)),
        in_specs=[SMEM] + [ANY] * 6,
        out_specs=(VMEM, VMEM),
        scratch_shapes=[
            basis_scratch,
            pltpu.VMEM((DATES, NF, paths), F32),
            pltpu.VMEM((K, trades), BF16),
            row_scratch,
            index_scratch,
            index_scratch,
            total_scratch,
            pltpu.SemaphoreType.DMA((5 + trades // TILE,)),
        ],
        compiler_params=params(),
        cost_estimate=pl.CostEstimate(
            flops=2 * 256 * 4096 * 1400, bytes_accessed=4 * 2**20, transcendentals=0
        ),
        name="values_and_sent_half",
    )(core, basis, fx_rates, coefficients, floor, group, names)
    received = lax.ppermute(send, "core", swap)
    total = pl.pallas_call(
        keep_kernel,
        out_shape=jax.ShapeDtypeStruct((OWNERS * HALF, DATES * paths), F32),
        in_specs=[SMEM, VMEM, ANY],
        out_specs=VMEM,
        scratch_shapes=[index_scratch, pltpu.SemaphoreType.DMA(())],
        compiler_params=params(),
        cost_estimate=pl.CostEstimate(
            flops=2 * 256 * 4096 * 1024, bytes_accessed=3 * 2**20, transcendentals=0
        ),
        name="kept_half",
    )(core, value, group)
    pair = pl.pallas_call(
        pair_kernel,
        out_shape=moment_shape,
        in_specs=[ANY, VMEM, VMEM],
        out_specs=ANY,
        scratch_shapes=[
            basis_scratch,
            pltpu.VMEM((OWNERS, HALF, LANES), F32),
            pltpu.SemaphoreType.DMA(()),
            pltpu.SemaphoreType.DMA((4,)),
        ],
        compiler_params=params(),
        name="pair_moments",
    )(basis, total, received)
    owned = lax.all_to_all(pair, ("x", "y"), 0, 0, tiled=True)

    far = lax.ppermute(near, "core", swap)
    inverse, wide = pl.pallas_call(
        inverse_kernel,
        out_shape=(
            jax.ShapeDtypeStruct((LANES, LANES), F32),
            jax.ShapeDtypeStruct((LANES, PATHS), BF16),
        ),
        in_specs=[VMEM] * 2,
        out_specs=(VMEM, VMEM),
        compiler_params=params(),
        cost_estimate=pl.CostEstimate(
            flops=2 * 2**31, bytes_accessed=2**21, transcendentals=0
        ),
        name="gram_inverse",
    )(near, far)

    summed = jnp.sum(owned, axis=0)
    inverse, summed = lax.optimization_barrier((inverse, summed))
    peers = lax.axis_size("z") * lax.axis_size("core")
    parts = lax.all_to_all(
        jnp.broadcast_to(summed[None], (peers, HALF, LANES)), ("z", "core"), 0, 0, tiled=True
    )
    exposure, expected = pl.pallas_call(
        exposure_kernel,
        out_shape=(
            jax.ShapeDtypeStruct((DATES, SET_DEV, paths), F32),
            jax.ShapeDtypeStruct((DATES, SET_DEV), F32),
        ),
        in_specs=[VMEM] * 4,
        out_specs=(VMEM, VMEM),
        compiler_params=params(),
        name="exposure",
    )(parts, inverse, basis, wide)
    return jnp.swapaxes(exposure, 1, 2), expected


def solution(mesh):
    parts = Mesh(mesh.devices.reshape(8, 2, 4, 8), ("z", "core", "x", "y"))
    path, trade = ("z", "core"), ("x", "y")
    return jax.shard_map(
        shards,
        mesh=parts,
        in_specs=(
            P(None, path, None),
            P(None, path, None),
            P(None, trade),
            P(trade),
            P(trade),
            P(trade),
        ),
        out_specs=(P(None, path, trade), P(None, trade)),
        check_vma=False,
    )
```

```python
import jax
import jax.numpy as jnp
from jax import lax
from jax.experimental import pallas as pl
from jax.experimental.pallas import tpu as pltpu
from jax.sharding import Mesh, PartitionSpec as P

F32 = jnp.float32
BF16 = jnp.bfloat16
HIGHEST = lax.Precision.HIGHEST
DATES = 2
K = 64
NF = 16
SETS = 2048
PATHS = 2048
OWNERS = 32
SET_DEV = SETS // OWNERS
HALF = SET_DEV // 2
LANES = DATES * K
TILE = 1024
VMEM = pl.BlockSpec(memory_space=pltpu.VMEM)
ANY = pl.BlockSpec(memory_space=pl.ANY)
SMEM = pl.BlockSpec(memory_space=pltpu.SMEM)


def split(x):
    high = x.astype(BF16)
    rest = x - high.astype(F32)
    middle = rest.astype(BF16)
    low = (rest - middle.astype(F32)).astype(BF16)
    return high, middle, low


def dot_nt(a, b, precision=None):
    return lax.dot_general(
        a, b, (((1,), (1,)), ((), ())), precision=precision, preferred_element_type=F32
    )


def dot_tn(a, b, precision=None):
    return lax.dot_general(
        a, b, (((0,), (0,)), ((), ())), precision=precision, preferred_element_type=F32
    )


def block_diagonal(a, b):
    return jnp.concatenate(
        [
            jnp.concatenate([a, jnp.zeros((a.shape[0], b.shape[1]), a.dtype)], axis=1),
            jnp.concatenate([jnp.zeros((b.shape[0], a.shape[1]), b.dtype), b], axis=1),
        ],
        axis=0,
    )


def net_half(half, value_ref, group_ref, total_ref):
    rows = OWNERS * HALF
    trades = value_ref.shape[1]
    for i in range(trades // TILE):
        span = pl.ds(i * TILE, TILE)
        group = group_ref[:, span]
        row = jnp.where(
            (group // HALF) % 2 == half, (group // SET_DEV) * HALF + group % HALF, -1
        )
        member = lax.broadcasted_iota(jnp.int32, (rows, TILE), 0) == row
        part = dot_nt(jnp.where(member, 1.0, 0.0).astype(BF16), value_ref[:, span])
        if i == 0:
            total_ref[...] = part
        else:
            total_ref[...] += part


def half_moments(wide, total_ref, store):
    step = 256
    for i in range(OWNERS * HALF // step):
        span = pl.ds(i * step, step)
        high, middle, low = split(total_ref[span, :])
        moments = (
            jnp.dot(high, wide, preferred_element_type=F32)
            + jnp.dot(middle, wide, preferred_element_type=F32)
            + jnp.dot(low, wide, preferred_element_type=F32)
        )
        store(i * step // HALF, moments.reshape(step // HALF, HALF, LANES))


def payload_kernel(basis_ref, out_ref, rows_ref, wide_ref, sems):
    wide_ref[...] = basis_ref[...].reshape(wide_ref.shape).astype(F32)
    copies = [
        pltpu.make_async_copy(wide_ref, out_ref.at[i], sems.at[i])
        for i in range(out_ref.shape[0])
    ]
    for copy in copies:
        copy.start()
    paths = wide_ref.shape[1]
    for d in range(DATES):
        rows_ref[d * paths : (d + 1) * paths, :] = wide_ref[d * K : (d + 1) * K, :].T.astype(BF16)
    for copy in copies:
        copy.wait()


def send_kernel(
    core_ref, basis_ref, fx_ref, coef_ref, floor_ref, group_ref, currency_ref,
    out_ref, value_ref, total_ref,
):
    trades = coef_ref.shape[1]
    basis = basis_ref[...]
    fx = jnp.concatenate([fx_ref[d].T for d in range(DATES)], axis=0)
    rates = jnp.concatenate(split(fx), axis=1)
    for i in range(trades // TILE):
        span = pl.ds(i * TILE, TILE)
        fitted = jnp.dot(basis, coef_ref[:, span], preferred_element_type=F32)
        names = lax.broadcasted_iota(jnp.int32, (3 * NF, TILE), 0) % NF
        chosen = jnp.where(names == currency_ref[:, span], 1.0, 0.0).astype(BF16)
        rate = jnp.dot(rates, chosen, preferred_element_type=F32)
        value_ref[:, span] = (rate * jnp.maximum(fitted, floor_ref[:, span])).astype(BF16)

    def store(at, moments):
        out_ref[pl.ds(at, moments.shape[0])] = moments

    net_half(1 - core_ref[0], value_ref, group_ref, total_ref)
    half_moments(by_date(basis), total_ref, store)


def keep_kernel(core_ref, value_ref, group_ref, total_ref):
    net_half(core_ref[0], value_ref, group_ref, total_ref)


def pair_kernel(basis_ref, total_ref, received_ref, out_hbm, sum_ref, sems):
    copies = []

    def store(at, moments):
        span = pl.ds(at, moments.shape[0])
        sum_ref[span] = moments + received_ref[span]
        copies.append(
            pltpu.make_async_copy(sum_ref.at[span], out_hbm.at[span], sems.at[len(copies)])
        )
        copies[-1].start()

    half_moments(by_date(basis_ref[...]), total_ref, store)
    for copy in copies:
        copy.wait()


def by_date(basis):
    paths = basis.shape[0] // DATES
    return block_diagonal(basis[:paths], basis[paths:])


def eliminate(blocks):
    row = lax.broadcasted_iota(jnp.int32, (8, LANES), 0)
    done = []
    for b in range(K // 8):
        height = K // 8 - b
        columns = [
            [
                jnp.broadcast_to(blocks[i][:, b * 8 + c : b * 8 + c + 1], (8, LANES))
                for i in range(b, K // 8)
            ]
            for c in range(8)
        ]
        rows = [blocks[b][c : c + 1, :] for c in range(8)]
        for c in range(8):
            pivot = columns[c][0][c : c + 1, :]
            inverse = 1.0 / pivot
            done.append(rows[c] * lax.rsqrt(pivot))
            scaled = rows[c] * inverse
            for e in range(c + 1, 8):
                entry = columns[c][0][e : e + 1, :]
                rows[e] = rows[e] - entry * scaled
                ratio = entry * inverse
                for i in range(height):
                    columns[e][i] = columns[e][i] - columns[c][i] * ratio
            for i in range(1, height):
                blocks[b + i] = blocks[b + i] - columns[c][i] * scaled
    return jnp.concatenate(done, axis=0)


def inverse_kernel(near_ref, far_ref, out_ref, wide_ref):
    groups = near_ref.shape[0]
    paths = near_ref.shape[2]
    gram = jnp.zeros((LANES, LANES), F32)
    for i, ref in enumerate((near_ref, far_ref)):
        for z in range(groups):
            at = (i * groups + z) * paths
            wide_ref[:, at : at + paths] = ref[z].astype(BF16)
    every = wide_ref[...]
    gram = dot_nt(every, every)
    row = lax.broadcasted_iota(jnp.int32, (K, K), 0)
    col = lax.broadcasted_iota(jnp.int32, (K, K), 1)
    eye = jnp.where(row == col, 1.0, 0.0).astype(F32)
    inverses = []
    for d in range(DATES):
        blocks = [
            jnp.concatenate(
                [gram[d * K + i : d * K + i + 8, d * K : d * K + K], eye[i : i + 8]], axis=1
            )
            for i in range(0, K, 8)
        ]
        factor_inverse = eliminate(blocks)[:, K:]
        inverses.append(dot_tn(factor_inverse, factor_inverse, HIGHEST))
    out_ref[...] = block_diagonal(*inverses)


def exposure_kernel(
    parts_ref, inverse_ref, basis_ref, wide_ref, exposure_ref, expected_ref
):
    peers = parts_ref.shape[0]
    halves = []
    for h in range(2):
        total = parts_ref[h]
        for i in range(h + 2, peers, 2):
            total = total + parts_ref[i]
        halves.append(total)
    moments = jnp.concatenate(halves, axis=0)
    beta = jnp.dot(moments, inverse_ref[...], precision=HIGHEST, preferred_element_type=F32)
    lane = lax.broadcasted_iota(jnp.int32, (SET_DEV, LANES), 1)
    rows = jnp.concatenate(
        [jnp.where(lane < K, beta, 0.0), jnp.where(lane < K, 0.0, beta)], axis=0
    )
    stacked = jnp.concatenate(split(rows), axis=0)

    def exposed(basis):
        smooth = jnp.dot(stacked, basis, preferred_element_type=F32)
        return jnp.maximum(
            smooth[:LANES] + smooth[LANES : 2 * LANES] + smooth[2 * LANES :], 0.0
        )

    paths = basis_ref.shape[2]
    exposure = exposed(basis_ref[...].reshape(LANES, paths))
    exposure_ref[...] = exposure.reshape(DATES, SET_DEV, paths)
    total = jnp.zeros((LANES, 128), F32)
    step = 512
    for i in range(PATHS // step):
        part = exposed(wide_ref[:, i * step : (i + 1) * step])
        for j in range(step // 128):
            total = total + part[:, j * 128 : (j + 1) * 128]
    mean = jnp.sum(total.T, axis=0, keepdims=True) / PATHS
    expected_ref[0:1, :] = mean[:, :SET_DEV]
    expected_ref[1:2, :] = mean[:, SET_DEV:]


def params(**more):
    return pltpu.CompilerParams(vmem_limit_bytes=40 * 2**20, **more)


def shards(basis, fx_rates, coefficients, unwind_worth_minimum, position_offset_group, currency):
    paths = basis.shape[1]
    trades = coefficients.shape[1]
    core = lax.axis_index("core").reshape(1)
    swap = [(0, 1), (1, 0)]
    floor = unwind_worth_minimum.reshape(1, trades)
    group = position_offset_group.reshape(1, trades)
    names = currency.reshape(1, trades)
    basis = jnp.swapaxes(basis, 1, 2)
    fx_rates = jnp.swapaxes(fx_rates, 1, 2)
    payload, rows = pl.pallas_call(
        payload_kernel,
        out_shape=(
            jax.ShapeDtypeStruct((lax.axis_size("z"), LANES, paths), F32),
            jax.ShapeDtypeStruct((DATES * paths, K), BF16),
        ),
        in_specs=[VMEM],
        out_specs=(ANY, VMEM),
        scratch_shapes=[
            pltpu.VMEM((LANES, paths), F32),
            pltpu.SemaphoreType.DMA((lax.axis_size("z"),)),
        ],
        compiler_params=params(),
        cost_estimate=pl.CostEstimate(flops=2**31, bytes_accessed=2**24, transcendentals=0),
        name="basis_payload",
    )(basis)
    near = lax.all_to_all(payload, "z", 0, 0, tiled=True)

    moment_shape = jax.ShapeDtypeStruct((OWNERS, HALF, LANES), F32)
    total_shape = (OWNERS * HALF, DATES * paths)
    send, value = pl.pallas_call(
        send_kernel,
        out_shape=(moment_shape, jax.ShapeDtypeStruct((DATES * paths, trades), BF16)),
        in_specs=[SMEM] + [VMEM] * 6,
        out_specs=(VMEM, VMEM),
        scratch_shapes=[pltpu.VMEM(total_shape, F32)],
        compiler_params=params(),
        cost_estimate=pl.CostEstimate(
            flops=2 * 256 * 4096 * 1400, bytes_accessed=4 * 2**20, transcendentals=0
        ),
        name="values_and_sent_half",
    )(core, rows, fx_rates, coefficients, floor, group, names)
    received = lax.ppermute(send, "core", swap)
    total = pl.pallas_call(
        keep_kernel,
        out_shape=jax.ShapeDtypeStruct(total_shape, F32),
        in_specs=[SMEM, VMEM, VMEM],
        out_specs=VMEM,
        compiler_params=params(),
        cost_estimate=pl.CostEstimate(
            flops=2 * 256 * 4096 * 1024, bytes_accessed=3 * 2**20, transcendentals=0
        ),
        name="kept_half",
    )(core, value, group)
    pair = pl.pallas_call(
        pair_kernel,
        out_shape=moment_shape,
        in_specs=[VMEM] * 3,
        out_specs=ANY,
        scratch_shapes=[
            pltpu.VMEM((OWNERS, HALF, LANES), F32),
            pltpu.SemaphoreType.DMA((4,)),
        ],
        compiler_params=params(),
        name="pair_moments",
    )(rows, total, received)
    owned = lax.all_to_all(pair, ("x", "y"), 0, 0, tiled=True)

    far = lax.ppermute(near, "core", swap)
    inverse, wide = pl.pallas_call(
        inverse_kernel,
        out_shape=(
            jax.ShapeDtypeStruct((LANES, LANES), F32),
            jax.ShapeDtypeStruct((LANES, PATHS), BF16),
        ),
        in_specs=[VMEM] * 2,
        out_specs=(VMEM, VMEM),
        compiler_params=params(),
        cost_estimate=pl.CostEstimate(
            flops=2 * 2**31, bytes_accessed=2**21, transcendentals=0
        ),
        name="gram_inverse",
    )(near, far)

    summed = jnp.sum(owned, axis=0)
    inverse, summed = lax.optimization_barrier((inverse, summed))
    peers = lax.axis_size("z") * lax.axis_size("core")
    parts = lax.all_to_all(
        jnp.broadcast_to(summed[None], (peers, HALF, LANES)), ("z", "core"), 0, 0, tiled=True
    )
    exposure, expected = pl.pallas_call(
        exposure_kernel,
        out_shape=(
            jax.ShapeDtypeStruct((DATES, SET_DEV, paths), F32),
            jax.ShapeDtypeStruct((DATES, SET_DEV), F32),
        ),
        in_specs=[VMEM] * 4,
        out_specs=(VMEM, VMEM),
        compiler_params=params(),
        name="exposure",
    )(parts, inverse, basis, wide)
    return jnp.swapaxes(exposure, 1, 2), expected


def solution(mesh):
    parts = Mesh(mesh.devices.reshape(8, 2, 4, 8), ("z", "core", "x", "y"))
    path, trade = ("z", "core"), ("x", "y")
    return jax.shard_map(
        shards,
        mesh=parts,
        in_specs=(
            P(None, path, None),
            P(None, path, None),
            P(None, trade),
            P(trade),
            P(trade),
            P(trade),
        ),
        out_specs=(P(None, path, trade), P(None, trade)),
        check_vma=False,
    )
```

```python
import jax
import jax.numpy as jnp
from jax import lax
from jax.experimental import pallas as pl
from jax.experimental.pallas import tpu as pltpu
from jax.sharding import Mesh, PartitionSpec as P

F32 = jnp.float32
BF16 = jnp.bfloat16
HIGHEST = lax.Precision.HIGHEST
DATES = 2
K = 64
NF = 16
SETS = 2048
PATHS = 2048
OWNERS = 32
SET_DEV = SETS // OWNERS
HALF = SET_DEV // 2
LANES = DATES * K
TILE = 1024
VMEM = pl.BlockSpec(memory_space=pltpu.VMEM)
ANY = pl.BlockSpec(memory_space=pl.ANY)
SMEM = pl.BlockSpec(memory_space=pltpu.SMEM)


def split(x):
    high = x.astype(BF16)
    rest = x - high.astype(F32)
    middle = rest.astype(BF16)
    low = (rest - middle.astype(F32)).astype(BF16)
    return high, middle, low


def dot_nt(a, b, precision=None):
    return lax.dot_general(
        a, b, (((1,), (1,)), ((), ())), precision=precision, preferred_element_type=F32
    )


def dot_tn(a, b, precision=None):
    return lax.dot_general(
        a, b, (((0,), (0,)), ((), ())), precision=precision, preferred_element_type=F32
    )


def block_diagonal(a, b):
    return jnp.concatenate(
        [
            jnp.concatenate([a, jnp.zeros((a.shape[0], b.shape[1]), a.dtype)], axis=1),
            jnp.concatenate([jnp.zeros((b.shape[0], a.shape[1]), b.dtype), b], axis=1),
        ],
        axis=0,
    )


def net_half(half, value_ref, group_ref, total_ref):
    rows = OWNERS * HALF
    trades = value_ref.shape[1]
    for i in range(trades // TILE):
        span = pl.ds(i * TILE, TILE)
        group = group_ref[:, span]
        row = jnp.where(
            (group // HALF) % 2 == half, (group // SET_DEV) * HALF + group % HALF, -1
        )
        member = lax.broadcasted_iota(jnp.int32, (rows, TILE), 0) == row
        part = dot_nt(jnp.where(member, 1.0, 0.0).astype(BF16), value_ref[:, span])
        if i == 0:
            total_ref[...] = part
        else:
            total_ref[...] += part


def half_moments(wide, total_ref, store):
    step = 256
    for i in range(OWNERS * HALF // step):
        span = pl.ds(i * step, step)
        high, middle, low = split(total_ref[span, :])
        moments = (
            jnp.dot(high, wide, preferred_element_type=F32)
            + jnp.dot(middle, wide, preferred_element_type=F32)
            + jnp.dot(low, wide, preferred_element_type=F32)
        )
        store(i * step // HALF, moments.reshape(step // HALF, HALF, LANES))


def payload_kernel(basis_ref, out_ref, rows_ref, wide_ref, sems):
    wide_ref[...] = basis_ref[...].reshape(wide_ref.shape).astype(F32)
    copies = [
        pltpu.make_async_copy(wide_ref, out_ref.at[i], sems.at[i])
        for i in range(out_ref.shape[0])
    ]
    for copy in copies:
        copy.start()
    paths = wide_ref.shape[1]
    for d in range(DATES):
        rows_ref[d * paths : (d + 1) * paths, :] = wide_ref[d * K : (d + 1) * K, :].T.astype(BF16)
    for copy in copies:
        copy.wait()


def send_kernel(
    core_ref, basis_ref, fx_ref, coef_ref, floor_ref, group_ref, currency_ref,
    out_ref, value_ref, total_ref,
):
    trades = coef_ref.shape[1]
    basis = basis_ref[...]
    fx = jnp.concatenate([fx_ref[d].T for d in range(DATES)], axis=0)
    rates = jnp.concatenate(split(fx), axis=1)
    for i in range(trades // TILE):
        span = pl.ds(i * TILE, TILE)
        fitted = jnp.dot(basis, coef_ref[:, span], preferred_element_type=F32)
        names = lax.broadcasted_iota(jnp.int32, (3 * NF, TILE), 0) % NF
        chosen = jnp.where(names == currency_ref[:, span], 1.0, 0.0).astype(BF16)
        rate = jnp.dot(rates, chosen, preferred_element_type=F32)
        value_ref[:, span] = (rate * jnp.maximum(fitted, floor_ref[:, span])).astype(BF16)

    def store(at, moments):
        out_ref[pl.ds(at, moments.shape[0])] = moments

    net_half(1 - core_ref[0], value_ref, group_ref, total_ref)
    half_moments(by_date(basis), total_ref, store)


def keep_kernel(core_ref, value_ref, group_ref, total_ref):
    net_half(core_ref[0], value_ref, group_ref, total_ref)


def pair_kernel(basis_ref, total_ref, received_ref, out_hbm, sum_ref, sems):
    copies = []

    def store(at, moments):
        span = pl.ds(at, moments.shape[0])
        sum_ref[span] = moments + received_ref[span]
        copies.append(
            pltpu.make_async_copy(sum_ref.at[span], out_hbm.at[span], sems.at[len(copies)])
        )
        copies[-1].start()

    half_moments(by_date(basis_ref[...]), total_ref, store)
    for copy in copies:
        copy.wait()


def by_date(basis):
    paths = basis.shape[0] // DATES
    return block_diagonal(basis[:paths], basis[paths:])


def eliminate(blocks):
    row = lax.broadcasted_iota(jnp.int32, (8, LANES), 0)
    done = []
    for b in range(K // 8):
        height = K // 8 - b
        columns = [
            [
                jnp.broadcast_to(blocks[i][:, b * 8 + c : b * 8 + c + 1], (8, LANES))
                for i in range(b, K // 8)
            ]
            for c in range(8)
        ]
        rows = [blocks[b][c : c + 1, :] for c in range(8)]
        for c in range(8):
            pivot = columns[c][0][c : c + 1, :]
            inverse = 1.0 / pivot
            done.append(rows[c] * lax.rsqrt(pivot))
            scaled = rows[c] * inverse
            for e in range(c + 1, 8):
                entry = columns[c][0][e : e + 1, :]
                rows[e] = rows[e] - entry * scaled
                ratio = entry * inverse
                for i in range(height):
                    columns[e][i] = columns[e][i] - columns[c][i] * ratio
            for i in range(1, height):
                blocks[b + i] = blocks[b + i] - columns[c][i] * scaled
    return jnp.concatenate(done, axis=0)


def inverse_kernel(near_ref, far_ref, out_ref, wide_ref):
    groups = near_ref.shape[0]
    paths = near_ref.shape[2]
    gram = jnp.zeros((LANES, LANES), F32)
    for i, ref in enumerate((near_ref, far_ref)):
        for z in range(groups):
            at = (i * groups + z) * paths
            wide_ref[:, at : at + paths] = ref[z].astype(BF16)
    every = wide_ref[...]
    gram = dot_nt(every, every)
    row = lax.broadcasted_iota(jnp.int32, (K, K), 0)
    col = lax.broadcasted_iota(jnp.int32, (K, K), 1)
    eye = jnp.where(row == col, 1.0, 0.0).astype(F32)
    inverses = []
    for d in range(DATES):
        blocks = [
            jnp.concatenate(
                [gram[d * K + i : d * K + i + 8, d * K : d * K + K], eye[i : i + 8]], axis=1
            )
            for i in range(0, K, 8)
        ]
        factor_inverse = eliminate(blocks)[:, K:]
        inverses.append(dot_tn(factor_inverse, factor_inverse, HIGHEST))
    out_ref[...] = block_diagonal(*inverses)


def exposure_kernel(
    halves_ref, inverse_ref, basis_ref, wide_ref, exposure_ref, expected_ref
):
    moments = halves_ref[...].reshape(SET_DEV, LANES)
    beta = jnp.dot(moments, inverse_ref[...], precision=HIGHEST, preferred_element_type=F32)
    lane = lax.broadcasted_iota(jnp.int32, (SET_DEV, LANES), 1)
    rows = jnp.concatenate(
        [jnp.where(lane < K, beta, 0.0), jnp.where(lane < K, 0.0, beta)], axis=0
    )
    stacked = jnp.concatenate(split(rows), axis=0)

    def exposed(basis):
        smooth = jnp.dot(stacked, basis, preferred_element_type=F32)
        return jnp.maximum(
            smooth[:LANES] + smooth[LANES : 2 * LANES] + smooth[2 * LANES :], 0.0
        )

    paths = basis_ref.shape[2]
    exposure = exposed(basis_ref[...].reshape(LANES, paths))
    exposure_ref[...] = exposure.reshape(DATES, SET_DEV, paths)
    total = jnp.zeros((LANES, 128), F32)
    step = 512
    for i in range(PATHS // step):
        part = exposed(wide_ref[:, i * step : (i + 1) * step])
        for j in range(step // 128):
            total = total + part[:, j * 128 : (j + 1) * 128]
    mean = jnp.sum(total.T, axis=0, keepdims=True) / PATHS
    expected_ref[0:1, :] = mean[:, :SET_DEV]
    expected_ref[1:2, :] = mean[:, SET_DEV:]


def params(**more):
    return pltpu.CompilerParams(vmem_limit_bytes=40 * 2**20, **more)


def shards(basis, fx_rates, coefficients, unwind_worth_minimum, position_offset_group, currency):
    paths = basis.shape[1]
    trades = coefficients.shape[1]
    core = lax.axis_index("core").reshape(1)
    swap = [(0, 1), (1, 0)]
    floor = unwind_worth_minimum.reshape(1, trades)
    group = position_offset_group.reshape(1, trades)
    names = currency.reshape(1, trades)
    basis = jnp.swapaxes(basis, 1, 2)
    fx_rates = jnp.swapaxes(fx_rates, 1, 2)
    payload, rows = pl.pallas_call(
        payload_kernel,
        out_shape=(
            jax.ShapeDtypeStruct((lax.axis_size("z"), LANES, paths), F32),
            jax.ShapeDtypeStruct((DATES * paths, K), BF16),
        ),
        in_specs=[VMEM],
        out_specs=(ANY, VMEM),
        scratch_shapes=[
            pltpu.VMEM((LANES, paths), F32),
            pltpu.SemaphoreType.DMA((lax.axis_size("z"),)),
        ],
        compiler_params=params(),
        cost_estimate=pl.CostEstimate(flops=2**31, bytes_accessed=2**24, transcendentals=0),
        name="basis_payload",
    )(basis)
    near = lax.all_to_all(payload, "z", 0, 0, tiled=True)

    moment_shape = jax.ShapeDtypeStruct((OWNERS, HALF, LANES), F32)
    total_shape = (OWNERS * HALF, DATES * paths)
    send, value = pl.pallas_call(
        send_kernel,
        out_shape=(moment_shape, jax.ShapeDtypeStruct((DATES * paths, trades), BF16)),
        in_specs=[SMEM] + [VMEM] * 6,
        out_specs=(VMEM, VMEM),
        scratch_shapes=[pltpu.VMEM(total_shape, F32)],
        compiler_params=params(),
        cost_estimate=pl.CostEstimate(
            flops=2 * 256 * 4096 * 1400, bytes_accessed=4 * 2**20, transcendentals=0
        ),
        name="values_and_sent_half",
    )(core, rows, fx_rates, coefficients, floor, group, names)
    received = lax.ppermute(send, "core", swap)
    total = pl.pallas_call(
        keep_kernel,
        out_shape=jax.ShapeDtypeStruct(total_shape, F32),
        in_specs=[SMEM, VMEM, VMEM],
        out_specs=VMEM,
        compiler_params=params(),
        cost_estimate=pl.CostEstimate(
            flops=2 * 256 * 4096 * 1024, bytes_accessed=3 * 2**20, transcendentals=0
        ),
        name="kept_half",
    )(core, value, group)
    pair = pl.pallas_call(
        pair_kernel,
        out_shape=moment_shape,
        in_specs=[VMEM] * 3,
        out_specs=ANY,
        scratch_shapes=[
            pltpu.VMEM((OWNERS, HALF, LANES), F32),
            pltpu.SemaphoreType.DMA((4,)),
        ],
        compiler_params=params(),
        name="pair_moments",
    )(rows, total, received)
    owned = lax.all_to_all(pair, ("x", "y"), 0, 0, tiled=True)

    far = lax.ppermute(near, "core", swap)
    inverse, wide = pl.pallas_call(
        inverse_kernel,
        out_shape=(
            jax.ShapeDtypeStruct((LANES, LANES), F32),
            jax.ShapeDtypeStruct((LANES, PATHS), BF16),
        ),
        in_specs=[VMEM] * 2,
        out_specs=(VMEM, VMEM),
        compiler_params=params(),
        cost_estimate=pl.CostEstimate(
            flops=2 * 2**31, bytes_accessed=2**21, transcendentals=0
        ),
        name="gram_inverse",
    )(near, far)

    summed = jnp.sum(owned, axis=0)
    inverse, summed = lax.optimization_barrier((inverse, summed))
    parts = lax.all_to_all(
        jnp.broadcast_to(summed[None], (lax.axis_size("z"), HALF, LANES)), "z", 0, 0, tiled=True
    )
    halves = lax.all_gather(jnp.sum(parts, axis=0), "core")
    exposure, expected = pl.pallas_call(
        exposure_kernel,
        out_shape=(
            jax.ShapeDtypeStruct((DATES, SET_DEV, paths), F32),
            jax.ShapeDtypeStruct((DATES, SET_DEV), F32),
        ),
        in_specs=[VMEM] * 4,
        out_specs=(VMEM, VMEM),
        compiler_params=params(),
        name="exposure",
    )(halves, inverse, basis, wide)
    return jnp.swapaxes(exposure, 1, 2), expected


def solution(mesh):
    parts = Mesh(mesh.devices.reshape(8, 2, 4, 8), ("z", "core", "x", "y"))
    path, trade = ("z", "core"), ("x", "y")
    return jax.shard_map(
        shards,
        mesh=parts,
        in_specs=(
            P(None, path, None),
            P(None, path, None),
            P(None, trade),
            P(trade),
            P(trade),
            P(trade),
        ),
        out_specs=(P(None, path, trade), P(None, trade)),
        check_vma=False,
    )
```

```python
import jax
import jax.numpy as jnp
from jax import lax
from jax.experimental import pallas as pl
from jax.experimental.pallas import tpu as pltpu
from jax.sharding import Mesh, PartitionSpec as P

F32 = jnp.float32
BF16 = jnp.bfloat16
HIGHEST = lax.Precision.HIGHEST
DATES = 2
K = 64
NF = 16
SETS = 2048
PATHS = 2048
OWNERS = 32
SET_DEV = SETS // OWNERS
HALF = SET_DEV // 2
LANES = DATES * K
TILE = 1024
VMEM = pl.BlockSpec(memory_space=pltpu.VMEM)
ANY = pl.BlockSpec(memory_space=pl.ANY)
SMEM = pl.BlockSpec(memory_space=pltpu.SMEM)


def split(x):
    high = x.astype(BF16)
    rest = x - high.astype(F32)
    middle = rest.astype(BF16)
    low = (rest - middle.astype(F32)).astype(BF16)
    return high, middle, low


def dot_nt(a, b, precision=None):
    return lax.dot_general(
        a, b, (((1,), (1,)), ((), ())), precision=precision, preferred_element_type=F32
    )


def dot_tn(a, b, precision=None):
    return lax.dot_general(
        a, b, (((0,), (0,)), ((), ())), precision=precision, preferred_element_type=F32
    )


def block_diagonal(a, b):
    return jnp.concatenate(
        [
            jnp.concatenate([a, jnp.zeros((a.shape[0], b.shape[1]), a.dtype)], axis=1),
            jnp.concatenate([jnp.zeros((b.shape[0], a.shape[1]), b.dtype), b], axis=1),
        ],
        axis=0,
    )


def net_half(half, value_ref, group_ref, total_ref):
    rows = OWNERS * HALF
    trades = value_ref.shape[1]
    for i in range(trades // TILE):
        span = pl.ds(i * TILE, TILE)
        group = group_ref[:, span]
        row = jnp.where(
            (group // HALF) % 2 == half, (group // SET_DEV) * HALF + group % HALF, -1
        )
        member = lax.broadcasted_iota(jnp.int32, (rows, TILE), 0) == row
        part = dot_nt(jnp.where(member, 1.0, 0.0).astype(BF16), value_ref[:, span])
        if i == 0:
            total_ref[...] = part
        else:
            total_ref[...] += part


def half_moments(wide, total_ref, store):
    step = 256
    for i in range(OWNERS * HALF // step):
        span = pl.ds(i * step, step)
        high, middle, low = split(total_ref[span, :])
        moments = (
            jnp.dot(high, wide, preferred_element_type=F32)
            + jnp.dot(middle, wide, preferred_element_type=F32)
            + jnp.dot(low, wide, preferred_element_type=F32)
        )
        store(i * step // HALF, moments.reshape(step // HALF, HALF, LANES))


def payload_kernel(basis_ref, out_ref, rows_ref):
    wide = basis_ref[...].reshape(out_ref.shape[1:]).astype(F32)
    for i in range(out_ref.shape[0]):
        out_ref[i] = wide
    paths = wide.shape[1]
    for d in range(DATES):
        rows_ref[d * paths : (d + 1) * paths, :] = wide[d * K : (d + 1) * K, :].T.astype(BF16)


def send_kernel(
    core_ref, basis_ref, fx_ref, coef_ref, floor_ref, group_ref, currency_ref,
    out_ref, value_ref, total_ref,
):
    trades = coef_ref.shape[1]
    basis = basis_ref[...]
    fx = jnp.concatenate([fx_ref[d].T for d in range(DATES)], axis=0)
    rates = jnp.concatenate(split(fx), axis=1)
    for i in range(trades // TILE):
        span = pl.ds(i * TILE, TILE)
        fitted = jnp.dot(basis, coef_ref[:, span], preferred_element_type=F32)
        names = lax.broadcasted_iota(jnp.int32, (3 * NF, TILE), 0) % NF
        chosen = jnp.where(names == currency_ref[:, span], 1.0, 0.0).astype(BF16)
        rate = jnp.dot(rates, chosen, preferred_element_type=F32)
        value_ref[:, span] = (rate * jnp.maximum(fitted, floor_ref[:, span])).astype(BF16)

    def store(at, moments):
        out_ref[pl.ds(at, moments.shape[0])] = moments

    net_half(1 - core_ref[0], value_ref, group_ref, total_ref)
    half_moments(by_date(basis), total_ref, store)


def keep_kernel(core_ref, value_ref, group_ref, total_ref):
    net_half(core_ref[0], value_ref, group_ref, total_ref)


def pair_kernel(basis_ref, total_ref, received_ref, out_ref):
    def store(at, moments):
        span = pl.ds(at, moments.shape[0])
        out_ref[span] = moments + received_ref[span]

    half_moments(by_date(basis_ref[...]), total_ref, store)


def by_date(basis):
    paths = basis.shape[0] // DATES
    return block_diagonal(basis[:paths], basis[paths:])


def eliminate(blocks):
    row = lax.broadcasted_iota(jnp.int32, (8, LANES), 0)
    done = []
    for b in range(K // 8):
        height = K // 8 - b
        columns = [
            [
                jnp.broadcast_to(blocks[i][:, b * 8 + c : b * 8 + c + 1], (8, LANES))
                for i in range(b, K // 8)
            ]
            for c in range(8)
        ]
        rows = [blocks[b][c : c + 1, :] for c in range(8)]
        for c in range(8):
            pivot = columns[c][0][c : c + 1, :]
            inverse = 1.0 / pivot
            done.append(rows[c] * lax.rsqrt(pivot))
            scaled = rows[c] * inverse
            for e in range(c + 1, 8):
                entry = columns[c][0][e : e + 1, :]
                rows[e] = rows[e] - entry * scaled
                ratio = entry * inverse
                for i in range(height):
                    columns[e][i] = columns[e][i] - columns[c][i] * ratio
            for i in range(1, height):
                blocks[b + i] = blocks[b + i] - columns[c][i] * scaled
    return jnp.concatenate(done, axis=0)


def inverse_kernel(near_ref, far_ref, out_ref, wide_ref):
    groups = near_ref.shape[0]
    paths = near_ref.shape[2]
    gram = jnp.zeros((LANES, LANES), F32)
    for i, ref in enumerate((near_ref, far_ref)):
        for z in range(groups):
            at = (i * groups + z) * paths
            wide_ref[:, at : at + paths] = ref[z].astype(BF16)
    every = wide_ref[...]
    gram = dot_nt(every, every)
    row = lax.broadcasted_iota(jnp.int32, (K, K), 0)
    col = lax.broadcasted_iota(jnp.int32, (K, K), 1)
    eye = jnp.where(row == col, 1.0, 0.0).astype(F32)
    inverses = []
    for d in range(DATES):
        blocks = [
            jnp.concatenate(
                [gram[d * K + i : d * K + i + 8, d * K : d * K + K], eye[i : i + 8]], axis=1
            )
            for i in range(0, K, 8)
        ]
        factor_inverse = eliminate(blocks)[:, K:]
        inverses.append(dot_tn(factor_inverse, factor_inverse, HIGHEST))
    out_ref[...] = block_diagonal(*inverses)


def exposure_kernel(
    halves_ref, inverse_ref, basis_ref, wide_ref, exposure_ref, expected_ref
):
    moments = halves_ref[...].reshape(SET_DEV, LANES)
    beta = jnp.dot(moments, inverse_ref[...], precision=HIGHEST, preferred_element_type=F32)
    lane = lax.broadcasted_iota(jnp.int32, (SET_DEV, LANES), 1)
    rows = jnp.concatenate(
        [jnp.where(lane < K, beta, 0.0), jnp.where(lane < K, 0.0, beta)], axis=0
    )
    high, middle, low = split(rows)
    upper = jnp.concatenate([high, middle], axis=1)

    def exposed(basis):
        twice = jnp.concatenate([basis, basis], axis=0)
        smooth = jnp.dot(upper, twice, preferred_element_type=F32)
        return jnp.maximum(smooth + jnp.dot(low, basis, preferred_element_type=F32), 0.0)

    paths = basis_ref.shape[2]
    exposure = exposed(basis_ref[...].reshape(LANES, paths))
    exposure_ref[...] = exposure.reshape(DATES, SET_DEV, paths)
    total = jnp.zeros((LANES, 128), F32)
    step = 256
    for i in range(PATHS // step):
        part = exposed(wide_ref[:, i * step : (i + 1) * step])
        for j in range(step // 128):
            total = total + part[:, j * 128 : (j + 1) * 128]
    mean = jnp.sum(total.T, axis=0, keepdims=True) / PATHS
    expected_ref[0:1, :] = mean[:, :SET_DEV]
    expected_ref[1:2, :] = mean[:, SET_DEV:]


def params(**more):
    return pltpu.CompilerParams(vmem_limit_bytes=40 * 2**20, **more)


def shards(basis, fx_rates, coefficients, unwind_worth_minimum, position_offset_group, currency):
    paths = basis.shape[1]
    trades = coefficients.shape[1]
    core = lax.axis_index("core").reshape(1)
    swap = [(0, 1), (1, 0)]
    floor = unwind_worth_minimum.reshape(1, trades)
    group = position_offset_group.reshape(1, trades)
    names = currency.reshape(1, trades)
    basis = jnp.swapaxes(basis, 1, 2)
    fx_rates = jnp.swapaxes(fx_rates, 1, 2)
    payload, rows = pl.pallas_call(
        payload_kernel,
        out_shape=(
            jax.ShapeDtypeStruct((lax.axis_size("z"), LANES, paths), F32),
            jax.ShapeDtypeStruct((DATES * paths, K), BF16),
        ),
        in_specs=[VMEM],
        out_specs=(VMEM, VMEM),
        compiler_params=params(),
        cost_estimate=pl.CostEstimate(flops=2**31, bytes_accessed=2**24, transcendentals=0),
        name="basis_payload",
    )(basis)
    near = lax.all_to_all(payload, "z", 0, 0, tiled=True)

    moment_shape = jax.ShapeDtypeStruct((OWNERS, HALF, LANES), F32)
    total_shape = (OWNERS * HALF, DATES * paths)
    send, value = pl.pallas_call(
        send_kernel,
        out_shape=(moment_shape, jax.ShapeDtypeStruct((DATES * paths, trades), BF16)),
        in_specs=[SMEM] + [VMEM] * 6,
        out_specs=(VMEM, VMEM),
        scratch_shapes=[pltpu.VMEM(total_shape, F32)],
        compiler_params=params(),
        cost_estimate=pl.CostEstimate(
            flops=2 * 256 * 4096 * 1400, bytes_accessed=4 * 2**20, transcendentals=0
        ),
        name="values_and_sent_half",
    )(core, rows, fx_rates, coefficients, floor, group, names)
    received = lax.ppermute(send, "core", swap)
    total = pl.pallas_call(
        keep_kernel,
        out_shape=jax.ShapeDtypeStruct(total_shape, F32),
        in_specs=[SMEM, VMEM, VMEM],
        out_specs=VMEM,
        compiler_params=params(),
        cost_estimate=pl.CostEstimate(
            flops=2 * 256 * 4096 * 1024, bytes_accessed=3 * 2**20, transcendentals=0
        ),
        name="kept_half",
    )(core, value, group)
    pair = pl.pallas_call(
        pair_kernel,
        out_shape=moment_shape,
        in_specs=[VMEM] * 3,
        out_specs=VMEM,
        compiler_params=params(),
        name="pair_moments",
    )(rows, total, received)
    owned = lax.all_to_all(pair, ("x", "y"), 0, 0, tiled=True)

    far = lax.ppermute(near, "core", swap)
    inverse, wide = pl.pallas_call(
        inverse_kernel,
        out_shape=(
            jax.ShapeDtypeStruct((LANES, LANES), F32),
            jax.ShapeDtypeStruct((LANES, PATHS), BF16),
        ),
        in_specs=[VMEM] * 2,
        out_specs=(VMEM, VMEM),
        compiler_params=params(),
        cost_estimate=pl.CostEstimate(
            flops=2 * 2**31, bytes_accessed=2**21, transcendentals=0
        ),
        name="gram_inverse",
    )(near, far)

    summed = jnp.sum(owned, axis=0)
    inverse, summed = lax.optimization_barrier((inverse, summed))
    parts = lax.all_to_all(
        jnp.broadcast_to(summed[None], (lax.axis_size("z"), HALF, LANES)), "z", 0, 0, tiled=True
    )
    halves = lax.all_gather(jnp.sum(parts, axis=0), "core")
    exposure, expected = pl.pallas_call(
        exposure_kernel,
        out_shape=(
            jax.ShapeDtypeStruct((DATES, SET_DEV, paths), F32),
            jax.ShapeDtypeStruct((DATES, SET_DEV), F32),
        ),
        in_specs=[VMEM] * 4,
        out_specs=(VMEM, VMEM),
        compiler_params=params(),
        name="exposure",
    )(halves, inverse, basis, wide)
    return jnp.swapaxes(exposure, 1, 2), expected


def solution(mesh):
    parts = Mesh(mesh.devices.reshape(8, 2, 4, 8), ("z", "core", "x", "y"))
    path, trade = ("z", "core"), ("x", "y")
    return jax.shard_map(
        shards,
        mesh=parts,
        in_specs=(
            P(None, path, None),
            P(None, path, None),
            P(None, trade),
            P(trade),
            P(trade),
            P(trade),
        ),
        out_specs=(P(None, path, trade), P(None, trade)),
        check_vma=False,
    )
```

```python
import jax
import jax.numpy as jnp
from jax import lax
from jax.experimental import pallas as pl
from jax.experimental.pallas import tpu as pltpu
from jax.sharding import Mesh, PartitionSpec as P

F32 = jnp.float32
BF16 = jnp.bfloat16
HIGHEST = lax.Precision.HIGHEST
DATES = 2
K = 64
NF = 16
SETS = 2048
PATHS = 2048
OWNERS = 32
SET_DEV = SETS // OWNERS
HALF = SET_DEV // 2
LANES = DATES * K
TILE = 1024
VMEM = pl.BlockSpec(memory_space=pltpu.VMEM)
ANY = pl.BlockSpec(memory_space=pl.ANY)
SMEM = pl.BlockSpec(memory_space=pltpu.SMEM)


def split(x):
    high = x.astype(BF16)
    rest = x - high.astype(F32)
    middle = rest.astype(BF16)
    low = (rest - middle.astype(F32)).astype(BF16)
    return high, middle, low


def dot_nt(a, b, precision=None):
    return lax.dot_general(
        a, b, (((1,), (1,)), ((), ())), precision=precision, preferred_element_type=F32
    )


def dot_tn(a, b, precision=None):
    return lax.dot_general(
        a, b, (((0,), (0,)), ((), ())), precision=precision, preferred_element_type=F32
    )


def block_diagonal(a, b):
    return jnp.concatenate(
        [
            jnp.concatenate([a, jnp.zeros((a.shape[0], b.shape[1]), a.dtype)], axis=1),
            jnp.concatenate([jnp.zeros((b.shape[0], a.shape[1]), b.dtype), b], axis=1),
        ],
        axis=0,
    )


def net_half(half, value_ref, group_ref, total_ref):
    rows = OWNERS * HALF
    trades = value_ref.shape[1]
    for i in range(trades // TILE):
        span = pl.ds(i * TILE, TILE)
        group = group_ref[:, span]
        row = jnp.where(
            (group // HALF) % 2 == half, (group // SET_DEV) * HALF + group % HALF, -1
        )
        member = lax.broadcasted_iota(jnp.int32, (rows, TILE), 0) == row
        part = dot_nt(jnp.where(member, 1.0, 0.0).astype(BF16), value_ref[:, span])
        if i == 0:
            total_ref[...] = part
        else:
            total_ref[...] += part


def half_moments(wide, total_ref, store):
    step = 256
    for i in range(OWNERS * HALF // step):
        span = pl.ds(i * step, step)
        high, middle, low = split(total_ref[span, :])
        moments = (
            jnp.dot(high, wide, preferred_element_type=F32)
            + jnp.dot(middle, wide, preferred_element_type=F32)
            + jnp.dot(low, wide, preferred_element_type=F32)
        )
        store(i * step // HALF, moments.reshape(step // HALF, HALF, LANES))


def payload_kernel(basis_ref, out_ref, rows_ref):
    wide = basis_ref[...]
    for i in range(out_ref.shape[0]):
        out_ref[i] = wide
    paths = wide.shape[1]
    for d in range(DATES):
        rows_ref[d * paths : (d + 1) * paths, :] = wide[d * K : (d + 1) * K, :].T.astype(BF16)


def send_kernel(
    core_ref, basis_ref, fx_ref, coef_ref, floor_ref, group_ref, currency_ref,
    out_ref, value_ref, total_ref,
):
    trades = coef_ref.shape[1]
    basis = basis_ref[...]
    fx = jnp.concatenate([fx_ref[d].T for d in range(DATES)], axis=0)
    rates = jnp.concatenate(split(fx), axis=1)
    for i in range(trades // TILE):
        span = pl.ds(i * TILE, TILE)
        fitted = jnp.dot(basis, coef_ref[:, span], preferred_element_type=F32)
        names = lax.broadcasted_iota(jnp.int32, (3 * NF, TILE), 0) % NF
        chosen = jnp.where(names == currency_ref[:, span], 1.0, 0.0).astype(BF16)
        rate = jnp.dot(rates, chosen, preferred_element_type=F32)
        value_ref[:, span] = (rate * jnp.maximum(fitted, floor_ref[:, span])).astype(BF16)

    def store(at, moments):
        out_ref[pl.ds(at, moments.shape[0])] = moments

    net_half(1 - core_ref[0], value_ref, group_ref, total_ref)
    half_moments(by_date(basis), total_ref, store)


def keep_kernel(core_ref, value_ref, group_ref, total_ref):
    net_half(core_ref[0], value_ref, group_ref, total_ref)


def pair_kernel(basis_ref, total_ref, received_ref, out_ref):
    def store(at, moments):
        span = pl.ds(at, moments.shape[0])
        out_ref[span] = moments + received_ref[span]

    half_moments(by_date(basis_ref[...]), total_ref, store)


def by_date(basis):
    paths = basis.shape[0] // DATES
    return block_diagonal(basis[:paths], basis[paths:])


def eliminate(blocks):
    row = lax.broadcasted_iota(jnp.int32, (8, LANES), 0)
    done = []
    for b in range(K // 8):
        height = K // 8 - b
        columns = [
            [
                jnp.broadcast_to(blocks[i][:, b * 8 + c : b * 8 + c + 1], (8, LANES))
                for i in range(b, K // 8)
            ]
            for c in range(8)
        ]
        rows = [blocks[b][c : c + 1, :] for c in range(8)]
        for c in range(8):
            pivot = columns[c][0][c : c + 1, :]
            inverse = 1.0 / pivot
            done.append(rows[c] * lax.rsqrt(pivot))
            scaled = rows[c] * inverse
            for e in range(c + 1, 8):
                entry = columns[c][0][e : e + 1, :]
                rows[e] = rows[e] - entry * scaled
                ratio = entry * inverse
                for i in range(height):
                    columns[e][i] = columns[e][i] - columns[c][i] * ratio
            for i in range(1, height):
                blocks[b + i] = blocks[b + i] - columns[c][i] * scaled
    return jnp.concatenate(done, axis=0)


def inverse_kernel(near_ref, far_ref, out_ref, wide_ref):
    groups = near_ref.shape[0]
    paths = near_ref.shape[2]
    gram = jnp.zeros((LANES, LANES), F32)
    for i, ref in enumerate((near_ref, far_ref)):
        for z in range(groups):
            at = (i * groups + z) * paths
            wide_ref[:, at : at + paths] = ref[z].astype(BF16)
    every = wide_ref[...]
    gram = dot_nt(every, every)
    row = lax.broadcasted_iota(jnp.int32, (K, K), 0)
    col = lax.broadcasted_iota(jnp.int32, (K, K), 1)
    eye = jnp.where(row == col, 1.0, 0.0).astype(F32)
    inverses = []
    for d in range(DATES):
        blocks = [
            jnp.concatenate(
                [gram[d * K + i : d * K + i + 8, d * K : d * K + K], eye[i : i + 8]], axis=1
            )
            for i in range(0, K, 8)
        ]
        factor_inverse = eliminate(blocks)[:, K:]
        inverses.append(dot_tn(factor_inverse, factor_inverse, HIGHEST))
    out_ref[...] = block_diagonal(*inverses)


def exposure_kernel(
    halves_ref, inverse_ref, basis_ref, wide_ref, exposure_ref, expected_ref
):
    moments = halves_ref[...].reshape(SET_DEV, LANES)
    beta = jnp.dot(moments, inverse_ref[...], precision=HIGHEST, preferred_element_type=F32)
    lane = lax.broadcasted_iota(jnp.int32, (SET_DEV, LANES), 1)
    rows = jnp.concatenate(
        [jnp.where(lane < K, beta, 0.0), jnp.where(lane < K, 0.0, beta)], axis=0
    )
    high, middle, low = split(rows)
    upper = jnp.concatenate([high, middle], axis=1)

    def exposed(basis):
        twice = jnp.concatenate([basis, basis], axis=0)
        smooth = jnp.dot(upper, twice, preferred_element_type=F32)
        return jnp.maximum(smooth + jnp.dot(low, basis, preferred_element_type=F32), 0.0)

    paths = basis_ref.shape[2]
    exposure = exposed(basis_ref[...].reshape(LANES, paths))
    exposure_ref[...] = exposure.reshape(DATES, SET_DEV, paths)
    total = jnp.zeros((LANES, 128), F32)
    step = 256
    for i in range(PATHS // step):
        part = exposed(wide_ref[:, i * step : (i + 1) * step])
        for j in range(step // 128):
            total = total + part[:, j * 128 : (j + 1) * 128]
    mean = jnp.sum(total.T, axis=0, keepdims=True) / PATHS
    expected_ref[0:1, :] = mean[:, :SET_DEV]
    expected_ref[1:2, :] = mean[:, SET_DEV:]


def params(**more):
    return pltpu.CompilerParams(vmem_limit_bytes=40 * 2**20, **more)


def shards(basis, fx_rates, coefficients, unwind_worth_minimum, position_offset_group, currency):
    paths = basis.shape[1]
    trades = coefficients.shape[1]
    core = lax.axis_index("core").reshape(1)
    swap = [(0, 1), (1, 0)]
    floor = unwind_worth_minimum.reshape(1, trades)
    group = position_offset_group.reshape(1, trades)
    names = currency.reshape(1, trades)
    basis = jnp.swapaxes(basis, 1, 2)
    fx_rates = jnp.swapaxes(fx_rates, 1, 2)
    payload, rows = pl.pallas_call(
        payload_kernel,
        out_shape=(
            jax.ShapeDtypeStruct((lax.axis_size("z"), LANES, paths), F32),
            jax.ShapeDtypeStruct((DATES * paths, K), BF16),
        ),
        grid=(1,),
        in_specs=[pl.BlockSpec((LANES, paths), lambda i: (0, 0))],
        out_specs=(VMEM, VMEM),
        compiler_params=params(allow_input_fusion=[True]),
        cost_estimate=pl.CostEstimate(flops=2**31, bytes_accessed=2**24, transcendentals=0),
        name="basis_payload",
    )(basis.reshape(LANES, paths).astype(F32))
    near = lax.all_to_all(payload, "z", 0, 0, tiled=True)

    moment_shape = jax.ShapeDtypeStruct((OWNERS, HALF, LANES), F32)
    total_shape = (OWNERS * HALF, DATES * paths)
    send, value = pl.pallas_call(
        send_kernel,
        out_shape=(moment_shape, jax.ShapeDtypeStruct((DATES * paths, trades), BF16)),
        in_specs=[SMEM] + [VMEM] * 6,
        out_specs=(VMEM, VMEM),
        scratch_shapes=[pltpu.VMEM(total_shape, F32)],
        compiler_params=params(),
        cost_estimate=pl.CostEstimate(
            flops=2 * 256 * 4096 * 1400, bytes_accessed=4 * 2**20, transcendentals=0
        ),
        name="values_and_sent_half",
    )(core, rows, fx_rates, coefficients, floor, group, names)
    received = lax.ppermute(send, "core", swap)
    total = pl.pallas_call(
        keep_kernel,
        out_shape=jax.ShapeDtypeStruct(total_shape, F32),
        in_specs=[SMEM, VMEM, VMEM],
        out_specs=VMEM,
        compiler_params=params(),
        cost_estimate=pl.CostEstimate(
            flops=2 * 256 * 4096 * 1024, bytes_accessed=3 * 2**20, transcendentals=0
        ),
        name="kept_half",
    )(core, value, group)
    pair = pl.pallas_call(
        pair_kernel,
        out_shape=moment_shape,
        in_specs=[VMEM] * 3,
        out_specs=VMEM,
        compiler_params=params(),
        name="pair_moments",
    )(rows, total, received)
    owned = lax.all_to_all(pair, ("x", "y"), 0, 0, tiled=True)

    far = lax.ppermute(near, "core", swap)
    inverse, wide = pl.pallas_call(
        inverse_kernel,
        out_shape=(
            jax.ShapeDtypeStruct((LANES, LANES), F32),
            jax.ShapeDtypeStruct((LANES, PATHS), BF16),
        ),
        in_specs=[VMEM] * 2,
        out_specs=(VMEM, VMEM),
        compiler_params=params(),
        cost_estimate=pl.CostEstimate(
            flops=2 * 2**31, bytes_accessed=2**21, transcendentals=0
        ),
        name="gram_inverse",
    )(near, far)

    summed = jnp.sum(owned, axis=0)
    inverse, summed = lax.optimization_barrier((inverse, summed))
    parts = lax.all_to_all(
        jnp.broadcast_to(summed[None], (lax.axis_size("z"), HALF, LANES)), "z", 0, 0, tiled=True
    )
    halves = lax.all_gather(jnp.sum(parts, axis=0), "core")
    exposure, expected = pl.pallas_call(
        exposure_kernel,
        out_shape=(
            jax.ShapeDtypeStruct((DATES, SET_DEV, paths), F32),
            jax.ShapeDtypeStruct((DATES, SET_DEV), F32),
        ),
        in_specs=[VMEM] * 4,
        out_specs=(VMEM, VMEM),
        compiler_params=params(),
        name="exposure",
    )(halves, inverse, basis, wide)
    return jnp.swapaxes(exposure, 1, 2), expected


def solution(mesh):
    parts = Mesh(mesh.devices.reshape(8, 2, 4, 8), ("z", "core", "x", "y"))
    path, trade = ("z", "core"), ("x", "y")
    return jax.shard_map(
        shards,
        mesh=parts,
        in_specs=(
            P(None, path, None),
            P(None, path, None),
            P(None, trade),
            P(trade),
            P(trade),
            P(trade),
        ),
        out_specs=(P(None, path, trade), P(None, trade)),
        check_vma=False,
    )
```
